128 devices in a mesh: sample: 8 (over z_hi, y), span: 16 (over x, z_lo, core).
Axes of the slice: x: 4, y: 4, z: 4 (z_hi: 2, z_lo: 2; z = z_hi * 2 + z_lo), core: 2. Of those that a mesh axis runs over, the one named last changes fastest.
Arguments:
- fields: float32 [3, 8, 128, 128, 193], P(None, 'sample', None, 'span'), may hold values from -1.5 to 1.5
- wiener: float32 [3, 8, 128, 128, 193], P(None, 'sample', None, 'span'), may hold values from -6 to 6
- velocity: float32 [3, 128, 128, 193], P(None, None, 'span'), may hold values from -6 to 6
- gradient: float32 [9, 128, 128, 193], P(None, None, 'span'), may hold values from -30 to 30
- wall_derivative: float32 [193, 193], replicated, may hold values from -4.2 to 4.2
- to_modes: float32 [193, 193], replicated, may hold values from -0.4375 to 0.4375
- from_modes: float32 [193, 193], replicated, may hold values from -0.4375 to 0.4375
- mode_rates: float32 [193], replicated, may hold values from 1 to 400
Outputs:
- new_fields: float32 [3, 8, 128, 128, 193], P(None, 'sample', None, 'span')
- new_velocity: float32 [3, 128, 128, 193], P(None, None, 'span')
- new_gradient: float32 [9, 128, 128, 193], P(None, None, 'span')
The draws below stay inside these ranges and needn't reach their ends.
All inputs are finite; a program needn't handle non-finite values.
Results may differ from the reference program's by a relative error of at most 0.0001.
Values sent between devices are 32-bit elements; how exact they have to be, the bound alone decides.
No kernel may reach another device: no remote copies, remote signals or barrier semaphores. Data moves between devices by JAX's collectives and lax.ppermute only.
A program may use at most 192 MiB of HBM per device.

```python
import math
import jax
import jax.numpy as jnp
from jax import lax

X = 128
Y = 193
Z = 128
FIELDS = 8


def level_of(stream_key, shape, split, least, top_value):
    def one(position, blocks):
        heights = jax.random.uniform(jax.random.fold_in(jax.random.fold_in(stream_key, 6), position), (blocks,), jnp.float32, least / len(split), top_value / len(split))
        return jnp.repeat(jnp.exp(heights), shape[position] // blocks).reshape((-1,) + (1,) * (len(shape) - position - 1))

    factor_of = one(*split[0])
    for cut in split[1:]:
        factor_of = factor_of * one(*cut)
    return factor_of


def centred(own_key, shape, deviation, limit, cuts=(), kind=jnp.bfloat16):
    drawn = deviation * jax.random.normal(own_key, shape, jnp.float32)
    if cuts:
        drawn = drawn * level_of(own_key, shape, cuts, -0.22, 0.18)
    return jnp.clip(drawn, -limit, limit).astype(kind)


def setup_inputs(seed: int = 0) -> dict:
    seeds = jax.random.split(jax.random.key(seed), 9)
    fields = jnp.clip(jax.random.uniform(seeds[0], (3, FIELDS, X, Z, Y), jnp.float32, -1.5, 1.5) * level_of(seeds[0], (3, FIELDS, X, Z, Y), ((1, 8), (3, 16)), -0.4, 0.0), -1.5, 1.5)
    wiener = centred(seeds[1], (3, FIELDS, X, Z, Y), 1.0, 6.0, ((1, 8), (3, 16)), jnp.float32)
    velocity = centred(seeds[2], (3, X, Z, Y), 1.0, 6.0, ((2, 16),), jnp.float32)
    gradient = centred(seeds[3], (9, X, Z, Y), 5.0, 30.0, ((2, 16),), jnp.float32)
    wall_derivative = centred(seeds[4], (Y, Y), 0.7, 4.2, (), jnp.float32)
    to_modes = centred(seeds[5], (Y, Y), Y ** -0.5, 0.4375, (), jnp.float32)
    from_modes = centred(seeds[6], (Y, Y), Y ** -0.5, 0.4375, (), jnp.float32)
    mode_rates = jnp.clip(jnp.exp(jax.random.uniform(seeds[7], (Y,), jnp.float32, math.log(1.0), math.log(400.0))), 1.0, 400.0)
    return {"fields": fields, "wiener": wiener, "velocity": velocity, "gradient": gradient, "wall_derivative": wall_derivative, "to_modes": to_modes, "from_modes": from_modes, "mode_rates": mode_rates}


TIME_STEP = 0.01
WEISSENBERG = 0.05
EXTENSIBILITY = 10.0
POLYMER_WEIGHT = 5.0
VISCOSITY = 0.5
DIFFUSIVITY = 0.003
LENGTH_X = math.pi
LENGTH_Z = 2.0 * math.pi / 3.0
PRECISE = lax.Precision.HIGHEST
FIRST_INDEX = (0, 0, 0, 1, 1, 2)
SECOND_INDEX = (0, 1, 2, 1, 2, 2)
IDENTITY_PAIRS = (1.0, 0.0, 0.0, 1.0, 0.0, 1.0)

def wave_numbers(period, extent, derivative):
    indices = jnp.arange(period)
    shifted = jnp.where(indices < period // 2, indices, indices - period)
    if derivative:
        shifted = jnp.where(indices == period // 2, 0, shifted)
    return shifted.astype(jnp.float32) * (2.0 * math.pi / extent)

def along_wall(values, wall_derivative):
    real_part = jnp.einsum('cxzy,wy->cxzw', values.real, wall_derivative, precision=PRECISE)
    imag_part = jnp.einsum('cxzy,wy->cxzw', values.imag, wall_derivative, precision=PRECISE)
    return real_part + 1j * imag_part

def apply_matrix(values, matrix):
    real_part = jnp.einsum('cxzy,wy->cxzw', values.real, matrix, precision=PRECISE)
    imag_part = jnp.einsum('cxzy,wy->cxzw', values.imag, matrix, precision=PRECISE)
    return real_part + 1j * imag_part

def reference(fields, wiener, velocity, gradient, wall_derivative, to_modes, from_modes, mode_rates):
    step_x = LENGTH_X / X
    step_z = LENGTH_Z / Z
    mean_square = lax.optimization_barrier(jnp.sum(fields * fields, axis=(0, 1))) / FIELDS
    spring = 1.0 / (1.0 - mean_square / EXTENSIBILITY)
    tensor = gradient.reshape(3, 3, X, Z, Y)
    noise_scale = math.sqrt(TIME_STEP / WEISSENBERG)
    curve_scale = DIFFUSIVITY * TIME_STEP / (step_z * step_z)

    def advance(moments, inputs):
        one_field, one_noise = inputs
        slope_x = (jnp.roll(one_field, -1, 1) - jnp.roll(one_field, 1, 1)) / (2.0 * step_x)
        slope_z = (jnp.roll(one_field, -1, 2) - jnp.roll(one_field, 1, 2)) / (2.0 * step_z)
        curve_z = jnp.roll(one_field, -1, 2) - 2.0 * one_field + jnp.roll(one_field, 1, 2)
        slope_y = jnp.einsum('cxzy,wy->cxzw', one_field, wall_derivative, precision=PRECISE)
        advect = velocity[0] * slope_x + velocity[1] * slope_y + velocity[2] * slope_z
        stretch = tensor[:, 0] * one_field[0] + tensor[:, 1] * one_field[1] + tensor[:, 2] * one_field[2]
        updated = one_field + TIME_STEP * (stretch - advect - spring * one_field / (2.0 * WEISSENBERG))
        updated = updated + curve_scale * curve_z + noise_scale * one_noise
        products = jnp.stack([updated[FIRST_INDEX[p]] * updated[SECOND_INDEX[p]] for p in range(6)])
        return (moments + products, updated)
    start = jnp.zeros((6, X, Z, Y), fields.dtype)
    moments, updated_all = lax.scan(advance, start, (jnp.moveaxis(fields, 1, 0), jnp.moveaxis(wiener, 1, 0)))
    new_fields = jnp.moveaxis(updated_all, 0, 1)
    identity = jnp.array(IDENTITY_PAIRS, fields.dtype)[:, None, None, None]
    stress = spring * (moments / FIELDS) - identity
    stacked = jnp.concatenate([stress, velocity], axis=0)
    spectra = jnp.fft.fft2(stacked, axes=(1, 2)) / (X * Z)
    kappa_x = wave_numbers(X, LENGTH_X, False)[None, :, None, None]
    kappa_z = wave_numbers(Z, LENGTH_Z, False)[None, None, :, None]
    slope_kx = wave_numbers(X, LENGTH_X, True)[None, :, None, None]
    slope_kz = wave_numbers(Z, LENGTH_Z, True)[None, None, :, None]
    column_x = spectra[0:3]
    column_y = jnp.stack([spectra[1], spectra[3], spectra[4]])
    column_z = jnp.stack([spectra[2], spectra[4], spectra[5]])
    divergence = 1j * slope_kx * column_x + along_wall(column_y, wall_derivative) + 1j * slope_kz * column_z
    forcing = spectra[6:9] + TIME_STEP * POLYMER_WEIGHT * divergence
    modes = apply_matrix(forcing, to_modes)
    damping = 1.0 + TIME_STEP * VISCOSITY * (kappa_x * kappa_x + kappa_z * kappa_z + mode_rates[None, None, None, :])
    velocity_hat = apply_matrix(modes / damping, from_modes)
    gradients = jnp.stack([1j * slope_kx * velocity_hat, along_wall(velocity_hat, wall_derivative), 1j * slope_kz * velocity_hat], axis=1)
    gradient_hat = gradients.reshape(9, X, Z, Y)
    combined = jnp.concatenate([velocity_hat, gradient_hat], axis=0)
    physical = (jnp.fft.ifft2(combined, axes=(1, 2)) * (X * Z)).real.astype(fields.dtype)
    return (new_fields, physical[0:3], physical[3:12])
```

```python
import math

import jax
import jax.numpy as jnp
import numpy as np
from jax import lax
from jax.sharding import PartitionSpec as P

TIME_STEP = 0.01
WEISSENBERG = 0.05
EXTENSIBILITY = 10.0
POLYMER_WEIGHT = 5.0
VISCOSITY = 0.5
DIFFUSIVITY = 0.003
LENGTH_X = math.pi
LENGTH_Z = 2.0 * math.pi / 3.0
FULL = lax.Precision.HIGHEST
HIGH = lax.Precision.HIGH
BOTH = ("sample", "span")


def real_basis(count, extent):
    half = count // 2
    place = np.arange(count)
    rows = np.zeros((count, count))
    kappa = np.zeros(count)
    slope = np.zeros((count, count))
    unit = 2.0 * math.pi / extent
    rows[0] = math.sqrt(1.0 / count)
    for k in range(1, half):
        angle = 2.0 * math.pi * ((k * place) % count) / count
        rows[k] = math.sqrt(2.0 / count) * np.cos(angle)
        rows[half + k] = math.sqrt(2.0 / count) * np.sin(angle)
        kappa[k] = kappa[half + k] = unit * k
        slope[k, half + k] = unit * k
        slope[half + k, k] = -unit * k
    rows[half] = math.sqrt(1.0 / count) * (1.0 - 2.0 * (place % 2))
    kappa[half] = unit * half
    return rows, slope, kappa * kappa


def f32(values):
    return jnp.asarray(np.asarray(values, np.float32))


def spring_free(fields, wiener, velocity, gradient, wall_derivative, step_x, step_z):
    span_count = lax.axis_size("span")
    ahead = [(i, (i + 1) % span_count) for i in range(span_count)]
    back = [((i + 1) % span_count, i) for i in range(span_count)]
    below = lax.ppermute(fields[:, :, -1:], "span", ahead)
    above = lax.ppermute(fields[:, :, :1], "span", back)
    upper = jnp.concatenate([fields[:, :, 1:], above], axis=2)
    lower = jnp.concatenate([below, fields[:, :, :-1]], axis=2)
    slope_z = (upper - lower) / (2.0 * step_z)
    curve_z = upper - 2.0 * fields + lower
    slope_x = (jnp.roll(fields, -1, axis=1) - jnp.roll(fields, 1, axis=1)) / (2.0 * step_x)
    slope_y = jnp.einsum("cxzy,wy->cxzw", fields, wall_derivative, precision=HIGH)
    advect = velocity[0] * slope_x + velocity[1] * slope_y + velocity[2] * slope_z
    tensor = gradient.reshape((3, 3) + gradient.shape[1:])
    stretch = tensor[:, 0] * fields[0] + tensor[:, 1] * fields[1] + tensor[:, 2] * fields[2]
    result = fields + TIME_STEP * (stretch - advect)
    result = result + DIFFUSIVITY * TIME_STEP / (step_z * step_z) * curve_z
    return result + math.sqrt(TIME_STEP / WEISSENBERG) * wiener


def gathered(plane, count):
    parts = [
        lax.ppermute(plane, "sample", [(i, (i + k) % count) for i in range(count)])
        for k in range(count - 1, 0, -1)
    ] + [plane]
    twice = jnp.stack(parts + parts)
    start = (count - 1 - lax.axis_index("sample")) % count
    return lax.dynamic_slice_in_dim(twice, start, count, axis=0)


def on_device(
    fields, wiener, velocity, gradient, wall_derivative, to_modes, from_modes, mode_rates
):
    size_x, slab, size_y = fields.shape[2:]
    samples = lax.axis_size("sample")
    spans = lax.axis_size("span")
    size_z = slab * spans
    step_x = LENGTH_X / size_x
    step_z = LENGTH_Z / size_z
    coupling = TIME_STEP * POLYMER_WEIGHT
    relax = TIME_STEP / (2.0 * WEISSENBERG)

    rows_x, slope_rows_x, square_x = real_basis(size_x, LENGTH_X)
    rows_z, slope_rows_z, square_z = real_basis(size_z, LENGTH_Z)
    order = np.array([slab * (d % spans) + d // spans for d in range(samples * spans)])

    field = fields[:, 0]
    field_planes = lax.all_to_all(
        jnp.transpose(field, (2, 0, 3, 1)), "sample", 0, 0, tiled=True
    )
    free = spring_free(
        field, wiener[:, 0], velocity, gradient, wall_derivative, step_x, step_z
    )
    free_planes = lax.all_to_all(
        jnp.transpose(free, (2, 0, 3, 1)), "sample", 0, 0, tiled=True
    )

    plane_square = jnp.sum(field_planes * field_planes, axis=(0, 1)) / samples
    spring = 1.0 / (1.0 - plane_square / EXTENSIBILITY)
    moved = free_planes - relax * spring * field_planes

    def stress(a, b):
        product = jnp.sum(moved[:, a] * moved[:, b], axis=0) / samples
        value = spring * product
        return value - 1.0 if a == b else value

    t00, t01, t02 = stress(0, 0), stress(0, 1), stress(0, 2)
    t11, t12, t22 = stress(1, 1), stress(1, 2), stress(2, 2)
    own_velocity = lax.dynamic_index_in_dim(
        velocity, lax.axis_index("sample"), 2, keepdims=False
    )
    modes_slope = coupling * jnp.dot(to_modes, wall_derivative, precision=FULL)
    modes_scaled = coupling * to_modes
    column_x = jnp.stack([t00, t01, t02])
    column_y = jnp.stack([t01, t11, t12])
    column_z = jnp.stack([t02, t12, t22])
    direct = jnp.einsum("my,cxy->cmx", to_modes, own_velocity, precision=FULL) + jnp.einsum(
        "my,cyx->cmx", modes_slope, column_y, precision=FULL
    )
    along_x = jnp.einsum("my,cyx->cmx", modes_scaled, column_x, precision=FULL)
    along_z = jnp.einsum("my,cyx->cmx", modes_scaled, column_z, precision=FULL)
    table_x = f32(np.concatenate([rows_x, slope_rows_x @ rows_x], axis=1))
    force = jnp.einsum(
        "rx,cmx->rcm", table_x, jnp.concatenate([direct, along_x], axis=2), precision=FULL
    )
    force_z = jnp.einsum("rx,cmx->rcm", f32(rows_x), along_z, precision=FULL)
    message = jnp.concatenate([force, force_z], axis=1)
    spectra = lax.all_to_all(message, BOTH, 0, 0, tiled=True)

    row = lax.axis_index("sample") * spans + lax.axis_index("span")
    square_row = lax.dynamic_index_in_dim(f32(square_x), row, 0, keepdims=False)
    table_f = f32(rows_z[:, order])
    table_g = f32((slope_rows_z @ rows_z)[:, order])
    solved = jnp.einsum("kz,zcm->kcm", table_f, spectra[:, :3], precision=FULL) + jnp.einsum(
        "kz,zcm->kcm", table_g, spectra[:, 3:], precision=FULL
    )
    damping = 1.0 + TIME_STEP * VISCOSITY * (
        square_row + f32(square_z)[:, None] + mode_rates[None, :]
    )
    solved = solved / damping[:, None, :]
    back_table = np.stack([rows_z.T, rows_z.T @ slope_rows_z]).reshape(2, spans, slab, size_z)
    back = jnp.einsum("dpzk,kcm->pdczm", f32(back_table), solved, precision=FULL)
    back, late_spring = lax.optimization_barrier((back, spring))
    slab_spring = gathered(late_spring, samples)
    back = jnp.broadcast_to(back[None], (samples,) + back.shape)
    back = back.reshape((samples * spans, 6, slab, size_y))
    rows = lax.all_to_all(back, BOTH, 0, 0, tiled=True)

    modes_wall = jnp.dot(wall_derivative, from_modes, precision=FULL)
    value = jnp.einsum("rczm,ym->rczy", rows, from_modes, precision=HIGH)
    value_y = jnp.einsum("rczm,ym->rczy", rows[:, :3], modes_wall, precision=HIGH)
    inverse = f32(rows_x.T)
    inverse_slope = f32(rows_x.T @ slope_rows_x)
    values = jnp.einsum("xr,rczy->cxzy", inverse, value, precision=HIGH)
    slope_x = jnp.einsum("xr,rczy->cxzy", inverse_slope, value[:, :3], precision=HIGH)
    slope_y = jnp.einsum("xr,rczy->cxzy", inverse, value_y, precision=HIGH)
    new_velocity = values[:3]
    new_gradient = jnp.stack([slope_x, slope_y, values[3:]], axis=1)
    new_gradient = new_gradient.reshape((9,) + new_gradient.shape[2:])

    new_fields = free - relax * jnp.transpose(slab_spring, (2, 0, 1)) * field
    return (new_fields[:, None], new_velocity, new_gradient)


def solution(mesh):
    in_specs = (
        P(None, "sample", None, "span", None),
        P(None, "sample", None, "span", None),
        P(None, None, "span", None),
        P(None, None, "span", None),
        P(),
        P(),
        P(),
        P(),
    )
    out_specs = (
        P(None, "sample", None, "span", None),
        P(None, None, "span", None),
        P(None, None, "span", None),
    )
    return jax.shard_map(
        on_device, mesh=mesh, in_specs=in_specs, out_specs=out_specs, check_vma=False
    )
```

```python
import functools
import math

import jax
import jax.numpy as jnp
import numpy as np
from jax import lax
from jax.experimental import pallas as pl
from jax.experimental.pallas import tpu as pltpu
from jax.sharding import PartitionSpec as P

TIME_STEP = 0.01
WEISSENBERG = 0.05
EXTENSIBILITY = 10.0
POLYMER_WEIGHT = 5.0
VISCOSITY = 0.5
DIFFUSIVITY = 0.003
LENGTH_X = math.pi
LENGTH_Z = 2.0 * math.pi / 3.0
FULL = lax.Precision.HIGHEST
HIGH = lax.Precision.HIGH
BOTH = ("sample", "span")
LANES = 256
PAIRS = ((0, 0), (0, 1), (0, 2), (1, 1), (1, 2), (2, 2))
COLUMN = ((0, 1, 2), (1, 3, 4), (2, 4, 5))


def real_basis(count, extent):
    half = count // 2
    place = np.arange(count)
    rows = np.zeros((count, count))
    kappa = np.zeros(count)
    slope = np.zeros((count, count))
    unit = 2.0 * math.pi / extent
    rows[0] = math.sqrt(1.0 / count)
    for k in range(1, half):
        angle = 2.0 * math.pi * ((k * place) % count) / count
        rows[k] = math.sqrt(2.0 / count) * np.cos(angle)
        rows[half + k] = math.sqrt(2.0 / count) * np.sin(angle)
        kappa[k] = kappa[half + k] = unit * k
        slope[k, half + k] = unit * k
        slope[half + k, k] = -unit * k
    rows[half] = math.sqrt(1.0 / count) * (1.0 - 2.0 * (place % 2))
    kappa[half] = unit * half
    return rows, slope, kappa * kappa


def f32(values):
    return jnp.asarray(np.asarray(values, np.float32))


def free_kernel(scales, f_ref, w_ref, v_ref, g_ref, lo_ref, hi_ref, d_ref, o_ref):
    scale_x, scale_z, scale_c, scale_w = scales
    i = pl.program_id(0)
    slab, _, size_y, size_x = f_ref.shape
    noise, speed, tensor = [
        r.reshape(r.shape[0], size_y * slab, size_x) for r in (w_ref, v_ref, g_ref)
    ]
    for z in range(slab):
        plane = pl.ds(z, size_y, stride=slab)
        own = f_ref[z, i]
        upper = hi_ref[i] if z == slab - 1 else f_ref[z + 1, i]
        lower = lo_ref[i] if z == 0 else f_ref[z - 1, i]
        slope_x = pltpu.roll(own, size_x - 1, 1) - pltpu.roll(own, 1, 1)
        slope_y = full_dot(d_ref[...], own)
        advect = (
            speed[0, plane, :] * (scale_x * slope_x)
            + speed[1, plane, :] * slope_y
            + speed[2, plane, :] * (scale_z * (upper - lower))
        )
        stretch = (
            tensor[0, plane, :] * f_ref[z, 0]
            + tensor[1, plane, :] * f_ref[z, 1]
            + tensor[2, plane, :] * f_ref[z, 2]
        )
        result = own + TIME_STEP * (stretch - advect)
        result = result + scale_c * (upper - 2.0 * own + lower)
        o_ref[z, 0] = result + scale_w * noise[0, plane, :]


def spring_free(planes, wiener, velocity, gradient, below, above, wall_derivative, step_x, step_z):
    slab, _, size_y, size_x = planes.shape
    whole = pl.BlockSpec(memory_space=pltpu.VMEM)
    scales = (
        1.0 / (2.0 * step_x),
        1.0 / (2.0 * step_z),
        DIFFUSIVITY * TIME_STEP / (step_z * step_z),
        math.sqrt(TIME_STEP / WEISSENBERG),
    )
    return pl.pallas_call(
        functools.partial(free_kernel, scales),
        grid=(3,),
        in_specs=[
            whole,
            pl.BlockSpec((1, size_y, slab, size_x), lambda i: (i, 0, 0, 0)),
            whole,
            pl.BlockSpec((3, size_y, slab, size_x), lambda i: (i, 0, 0, 0)),
            whole,
            whole,
            whole,
        ],
        out_specs=pl.BlockSpec((slab, 1, size_y, size_x), lambda i: (0, i, 0, 0)),
        out_shape=pltpu.HBM(planes.shape, jnp.float32),
        compiler_params=pltpu.CompilerParams(vmem_limit_bytes=32 * 1024 * 1024),
        cost_estimate=pl.CostEstimate(flops=3 * 10**9, bytes_accessed=18 * 10**6, transcendentals=0),
    )(planes, wiener, velocity, gradient, below, above, wall_derivative)


def padded(values, rows, columns):
    return jnp.pad(
        values, ((0, rows - values.shape[0]), (0, columns - values.shape[1]))
    )


def stacked_three(table):
    table = np.asarray(table, np.float32)
    high = table.astype(jnp.bfloat16)
    low = (table - high.astype(np.float32)).astype(jnp.bfloat16)
    return jnp.asarray(np.concatenate([high, high, low], axis=0))


def split_three(table, axis):
    high = lax.reduce_precision(table, 8, 7)
    low = (table - high).astype(jnp.bfloat16)
    high = high.astype(jnp.bfloat16)
    return jnp.concatenate([high, high, low], axis=axis)


def three_of(values, axis):
    high = values.astype(jnp.bfloat16)
    low = (values - high.astype(jnp.float32)).astype(jnp.bfloat16)
    return jnp.concatenate([high, low, high], axis=axis)


def full_dot(a, b, side=0):
    return lax.dot_general(
        a,
        b,
        (((1,), (side,)), ((), ())),
        precision=FULL,
        preferred_element_type=jnp.float32,
    )


def plane_kernel(coupling, relax, f_ref, a_ref, s_ref, v_ref, m_ref, x_ref, o_ref, t_ref):
    count, _, size_y, size_x = f_ref.shape
    for start in range(0, size_y, 32):
        part = pl.ds(start, min(32, size_y - start))
        spring = s_ref[part, :]
        scale = relax * spring
        sums = [None] * 6
        for k in range(count):
            moved = [a_ref[k, c, part, :] - scale * f_ref[k, c, part, :] for c in range(3)]
            for p, (i, j) in enumerate(PAIRS):
                value = moved[i] * moved[j]
                sums[p] = value if sums[p] is None else sums[p] + value
        for p, (i, j) in enumerate(PAIRS):
            value = spring * (sums[p] / count)
            t_ref[p, part, :] = value - 1.0 if i == j else value
    modes, slope = m_ref[:LANES, :], m_ref[LANES:, :]
    scaled = coupling * modes
    rows, slope_rows = x_ref[:size_x, :], x_ref[size_x:, :]
    for i in range(3):
        direct = full_dot(modes, v_ref[i]) + full_dot(slope, t_ref[COLUMN[i][1]])
        along_x = full_dot(scaled, t_ref[COLUMN[i][0]])
        along_z = full_dot(scaled, t_ref[COLUMN[i][2]])
        force = full_dot(rows, direct, 1) + full_dot(slope_rows, along_x, 1)
        force_z = full_dot(rows, along_z, 1)
        for half in range(2):
            lanes = slice(half * 128, half * 128 + 128)
            o_ref[pl.ds(8 * half + i, 128, stride=16), :] = force[:, lanes]
            o_ref[pl.ds(8 * half + 3 + i, 128, stride=16), :] = force_z[:, lanes]


def own_plane(field_planes, free_planes, spring, own_velocity, modes, rows, coupling, relax):
    _, _, size_y, size_x = field_planes.shape
    message = pl.pallas_call(
        functools.partial(plane_kernel, coupling, relax),
        out_shape=jax.ShapeDtypeStruct((size_x * 16, 128), jnp.float32),
        scratch_shapes=[pltpu.VMEM((6, size_y, size_x), jnp.float32)],
        compiler_params=pltpu.CompilerParams(vmem_limit_bytes=60 * 1024 * 1024),
    )(field_planes, free_planes, spring, own_velocity, modes, rows)
    return message.reshape(size_x, 2, 8, 128)


def row_kernel(spans, in_ref, d_ref, f_ref, g_ref, b_ref, o_ref, t_ref, sem):
    flat = in_ref.reshape(in_ref.shape[0] * 16, 128)
    lane = lax.broadcasted_iota(jnp.int32, (128, 128), 1)
    last = jnp.zeros((128, 128), jnp.float32)

    def loaded(c):
        return jnp.concatenate(
            [flat[pl.ds(8 * half + c, 128, stride=16), :] for half in range(2)], axis=1
        )

    for i in range(3):
        solved = full_dot(f_ref[...], loaded(i)) + full_dot(g_ref[...], loaded(3 + i))
        both = full_dot(b_ref[...], solved / d_ref[...])
        value, slope = both[:128], both[128:]
        t_ref[:, i] = value[:, :128].reshape(spans, 8, 128)
        t_ref[:, 3 + i] = slope[:, :128].reshape(spans, 8, 128)
        value, slope = value[:, 128:], slope[:, 128:]
        mixed = jnp.where(lane < 64, value, pltpu.roll(slope, 64, 1))
        t_ref[:, 6 + i] = mixed.reshape(spans, 8, 128)
        last = jnp.where(lane == i, pltpu.roll(value, 64 + i, 1), last)
        last = jnp.where(lane == 3 + i, pltpu.roll(slope, 67 + i, 1), last)
    t_ref[:, 9] = last.reshape(spans, 8, 128)
    copies = [
        pltpu.make_async_copy(t_ref, o_ref.at[pl.ds(k * spans, spans)], sem.at[k])
        for k in range(o_ref.shape[0] // spans)
    ]
    for copy in copies:
        copy.start()
    for copy in copies:
        copy.wait()


def own_row(spectra, damping, forward, forward_slope, inverse, samples, spans):
    whole = pl.BlockSpec(memory_space=pltpu.VMEM)
    return pl.pallas_call(
        functools.partial(row_kernel, spans),
        in_specs=[whole] * 5,
        out_specs=pl.BlockSpec(memory_space=pltpu.HBM),
        out_shape=pltpu.HBM((samples * spans, 10, 8, 128), jnp.float32),
        scratch_shapes=[
            pltpu.VMEM((spans, 10, 8, 128), jnp.float32),
            pltpu.SemaphoreType.DMA((samples,)),
        ],
        compiler_params=pltpu.CompilerParams(vmem_limit_bytes=32 * 1024 * 1024),
    )(spectra, damping, forward, forward_slope, inverse)


def slab_kernel(u_ref, w_ref, h_ref, l_ref, t_ref, x_ref, v_ref, g_ref):
    i = pl.program_id(0)
    rows = u_ref.shape[0]
    _, size_y, slab, size_x = v_ref.shape
    flat = [r.reshape(rows * slab, 128) for r in (u_ref, w_ref, h_ref, l_ref)]
    out_v = v_ref.reshape(size_y * slab, size_x)
    out_g = g_ref.reshape(3, size_y * slab, size_x)
    lane = lax.broadcasted_iota(jnp.int32, (rows, 128), 1)
    half = t_ref.shape[0] // 2
    for first in range(0, slab, 2):
        values, slopes = [], []
        for z in (first, first + 1):
            value, slope, high, last = [r[pl.ds(z, rows, stride=slab), :] for r in flat]
            value_high = jnp.where(lane < 64, high, pltpu.roll(last, 64 - i, 1))
            slope_high = jnp.where(
                lane < 64, pltpu.roll(high, 64, 1), pltpu.roll(last, 61 - i, 1)
            )
            value_high = jnp.where(lane <= 64, value_high, 0.0)
            slope_high = jnp.where(lane <= 64, slope_high, 0.0)
            values.append(jnp.concatenate([value, value_high], axis=1))
            slopes.append(jnp.concatenate([slope, slope_high], axis=1))
        across = (((1,), (1,)), ((), ()))
        value = lax.dot_general(
            t_ref[...],
            three_of(jnp.concatenate(values, axis=0), 1),
            across,
            preferred_element_type=jnp.float32,
        )
        slope = lax.dot_general(
            t_ref[:half],
            three_of(jnp.concatenate(slopes, axis=0), 1),
            across,
            preferred_element_type=jnp.float32,
        )
        for k, z in enumerate((first, first + 1)):
            place = pl.ds(z, size_y, stride=slab)
            lanes = slice(k * rows, k * rows + rows)
            both = jnp.dot(
                three_of(value[:half, lanes], 1), x_ref[...], preferred_element_type=jnp.float32
            )
            out_v[place, :] = both[:size_y, :size_x]
            out_g[0, place, :] = both[:size_y, size_x:]
            both = jnp.dot(
                three_of(jnp.concatenate([value[half:, lanes], slope[:, lanes]], axis=0), 1),
                x_ref[:, :size_x],
                preferred_element_type=jnp.float32,
            )
            out_g[1, place, :] = both[:size_y]
            out_g[2, place, :] = both[half : half + size_y]


def slab_values(rows, wall_table, table_x, size_y):
    count = rows.shape[0]
    slab, size_x = rows.shape[2], table_x.shape[1] // 2
    whole = pl.BlockSpec(memory_space=pltpu.VMEM)

    def piece(place):
        return pl.BlockSpec((count, 1, slab, 128), lambda i: (0, place(i), 0, 0))

    return pl.pallas_call(
        slab_kernel,
        grid=(3,),
        in_specs=[
            piece(lambda i: i),
            piece(lambda i: i + 3),
            piece(lambda i: i + 6),
            piece(lambda i: 9),
            whole,
            whole,
        ],
        out_specs=(
            pl.BlockSpec((1, size_y, slab, size_x), lambda i: (i, 0, 0, 0)),
            pl.BlockSpec((3, size_y, slab, size_x), lambda i: (i, 0, 0, 0)),
        ),
        out_shape=(
            jax.ShapeDtypeStruct((3, size_y, slab, size_x), jnp.float32),
            jax.ShapeDtypeStruct((9, size_y, slab, size_x), jnp.float32),
        ),
        compiler_params=pltpu.CompilerParams(vmem_limit_bytes=60 * 1024 * 1024),
    )(rows, rows, rows, rows, wall_table, table_x)


def gathered(plane, count):
    index = lax.axis_index("sample")
    ring = count // 2
    parts = [
        lax.ppermute(
            plane,
            "sample",
            [(i, i - i % ring + (i + k) % ring) for i in range(count)],
        )
        for k in range(ring - 1, 0, -1)
    ] + [plane]
    start = (ring - 1 - index % ring) % ring
    planes = lax.dynamic_slice_in_dim(jnp.stack(parts + parts), start, ring, axis=0)
    other = lax.ppermute(planes, "sample", [(i, (i + ring) % count) for i in range(count)])
    return jnp.where(
        index < ring,
        jnp.concatenate([planes, other]),
        jnp.concatenate([other, planes]),
    )


def on_device(
    fields, wiener, velocity, gradient, wall_derivative, to_modes, from_modes, mode_rates
):
    size_x, slab, size_y = fields.shape[2:]
    samples = lax.axis_size("sample")
    spans = lax.axis_size("span")
    size_z = slab * spans
    step_x = LENGTH_X / size_x
    step_z = LENGTH_Z / size_z
    coupling = TIME_STEP * POLYMER_WEIGHT
    relax = TIME_STEP / (2.0 * WEISSENBERG)

    rows_x, slope_rows_x, square_x = real_basis(size_x, LENGTH_X)
    rows_z, slope_rows_z, square_z = real_basis(size_z, LENGTH_Z)
    order = np.array([slab * (d % spans) + d // spans for d in range(samples * spans)])

    field = jnp.transpose(fields[:, 0], (2, 0, 3, 1))
    ahead = [(i, (i + 1) % spans) for i in range(spans)]
    back = [((i + 1) % spans, i) for i in range(spans)]
    below = lax.ppermute(field[-1], "span", ahead)
    above = lax.ppermute(field[0], "span", back)
    field_planes = lax.all_to_all(field, "sample", 0, 0, tiled=True)
    speed = jnp.transpose(velocity, (0, 3, 2, 1))
    free = spring_free(
        field,
        jnp.transpose(wiener[:, 0], (0, 3, 2, 1)),
        speed,
        jnp.transpose(gradient, (0, 3, 2, 1)),
        below,
        above,
        wall_derivative,
        step_x,
        step_z,
    )
    free_planes = lax.all_to_all(free, "sample", 0, 0, tiled=True)

    own_velocity = lax.dynamic_index_in_dim(
        speed, lax.axis_index("sample"), 2, keepdims=False
    )
    modes = padded(to_modes, LANES, size_y)
    modes_slope = coupling * jnp.dot(modes, wall_derivative, precision=FULL)
    plane_square = jnp.sum(field_planes * field_planes, axis=(0, 1)) / samples
    spring = 1.0 / (1.0 - plane_square / EXTENSIBILITY)
    slab_spring = gathered(spring, samples)
    message = own_plane(
        field_planes,
        free_planes,
        spring,
        own_velocity,
        jnp.concatenate([modes, modes_slope]),
        f32(np.concatenate([rows_x, slope_rows_x @ rows_x])),
        coupling,
        relax,
    )
    message, slab_spring = lax.optimization_barrier((message, slab_spring))
    spectra = lax.all_to_all(message, BOTH, 0, 0, tiled=True)

    row = lax.axis_index("sample") * spans + lax.axis_index("span")
    square_row = lax.dynamic_index_in_dim(f32(square_x), row, 0, keepdims=False)
    rates = padded(mode_rates[None, :], 1, LANES)
    damping = 1.0 + TIME_STEP * VISCOSITY * (
        square_row + f32(square_z)[:, None] + rates
    )
    back = own_row(
        spectra,
        damping,
        f32(rows_z[:, order]),
        f32((slope_rows_z @ rows_z)[:, order]),
        f32(np.concatenate([rows_z.T, rows_z.T @ slope_rows_z])),
        samples,
        spans,
    )
    rows = lax.all_to_all(back, BOTH, 0, 0, tiled=True)

    modes_wall = jnp.dot(wall_derivative, from_modes, precision=FULL)
    wall_table = jnp.concatenate(
        [padded(from_modes, 208, LANES), padded(modes_wall, 208, LANES)]
    )
    new_velocity, new_gradient = slab_values(
        rows,
        split_three(wall_table, 1),
        stacked_three(np.concatenate([rows_x, (rows_x.T @ slope_rows_x).T], axis=1)),
        size_y,
    )
    new_fields = free - relax * slab_spring[:, None] * field
    return (
        jnp.transpose(new_fields, (1, 3, 0, 2))[:, None],
        jnp.transpose(new_velocity, (0, 3, 2, 1)),
        jnp.transpose(new_gradient, (0, 3, 2, 1)),
    )


def solution(mesh):
    in_specs = (
        P(None, "sample", None, "span", None),
        P(None, "sample", None, "span", None),
        P(None, None, "span", None),
        P(None, None, "span", None),
        P(),
        P(),
        P(),
        P(),
    )
    out_specs = (
        P(None, "sample", None, "span", None),
        P(None, None, "span", None),
        P(None, None, "span", None),
    )
    return jax.shard_map(
        on_device, mesh=mesh, in_specs=in_specs, out_specs=out_specs, check_vma=False
    )
```

```python
import functools
import math

import jax
import jax.numpy as jnp
import numpy as np
from jax import lax
from jax.experimental import pallas as pl
from jax.experimental.pallas import tpu as pltpu
from jax.sharding import PartitionSpec as P

TIME_STEP = 0.01
WEISSENBERG = 0.05
EXTENSIBILITY = 10.0
POLYMER_WEIGHT = 5.0
VISCOSITY = 0.5
DIFFUSIVITY = 0.003
LENGTH_X = math.pi
LENGTH_Z = 2.0 * math.pi / 3.0
FULL = lax.Precision.HIGHEST
HIGH = lax.Precision.HIGH
BOTH = ("sample", "span")
LANES = 256
PAIRS = ((0, 0), (0, 1), (0, 2), (1, 1), (1, 2), (2, 2))
COLUMN = ((0, 1, 2), (1, 3, 4), (2, 4, 5))


def real_basis(count, extent):
    half = count // 2
    place = np.arange(count)
    rows = np.zeros((count, count))
    kappa = np.zeros(count)
    slope = np.zeros((count, count))
    unit = 2.0 * math.pi / extent
    rows[0] = math.sqrt(1.0 / count)
    for k in range(1, half):
        angle = 2.0 * math.pi * ((k * place) % count) / count
        rows[k] = math.sqrt(2.0 / count) * np.cos(angle)
        rows[half + k] = math.sqrt(2.0 / count) * np.sin(angle)
        kappa[k] = kappa[half + k] = unit * k
        slope[k, half + k] = unit * k
        slope[half + k, k] = -unit * k
    rows[half] = math.sqrt(1.0 / count) * (1.0 - 2.0 * (place % 2))
    kappa[half] = unit * half
    return rows, slope, kappa * kappa


def f32(values):
    return jnp.asarray(np.asarray(values, np.float32))


def free_kernel(scales, f_ref, w_ref, v_ref, g_ref, lo_ref, hi_ref, d_ref, o_ref):
    scale_x, scale_z, scale_c, scale_w = scales
    i = pl.program_id(0)
    slab, _, size_y, size_x = f_ref.shape
    noise, speed, tensor = [
        r.reshape(r.shape[0], size_y * slab, size_x) for r in (w_ref, v_ref, g_ref)
    ]
    for z in range(slab):
        plane = pl.ds(z, size_y, stride=slab)
        own = f_ref[z, i]
        upper = hi_ref[i] if z == slab - 1 else f_ref[z + 1, i]
        lower = lo_ref[i] if z == 0 else f_ref[z - 1, i]
        slope_x = pltpu.roll(own, size_x - 1, 1) - pltpu.roll(own, 1, 1)
        slope_y = full_dot(d_ref[...], own)
        advect = (
            speed[0, plane, :] * (scale_x * slope_x)
            + speed[1, plane, :] * slope_y
            + speed[2, plane, :] * (scale_z * (upper - lower))
        )
        stretch = (
            tensor[0, plane, :] * f_ref[z, 0]
            + tensor[1, plane, :] * f_ref[z, 1]
            + tensor[2, plane, :] * f_ref[z, 2]
        )
        result = own + TIME_STEP * (stretch - advect)
        result = result + scale_c * (upper - 2.0 * own + lower)
        o_ref[z, 0] = result + scale_w * noise[0, plane, :]


def spring_free(planes, wiener, velocity, gradient, below, above, wall_derivative, step_x, step_z):
    slab, _, size_y, size_x = planes.shape
    whole = pl.BlockSpec(memory_space=pltpu.VMEM)
    scales = (
        1.0 / (2.0 * step_x),
        1.0 / (2.0 * step_z),
        DIFFUSIVITY * TIME_STEP / (step_z * step_z),
        math.sqrt(TIME_STEP / WEISSENBERG),
    )
    return pl.pallas_call(
        functools.partial(free_kernel, scales),
        grid=(3,),
        in_specs=[
            whole,
            pl.BlockSpec((1, size_y, slab, size_x), lambda i: (i, 0, 0, 0)),
            whole,
            pl.BlockSpec((3, size_y, slab, size_x), lambda i: (i, 0, 0, 0)),
            whole,
            whole,
            whole,
        ],
        out_specs=pl.BlockSpec((slab, 1, size_y, size_x), lambda i: (0, i, 0, 0)),
        out_shape=pltpu.HBM(planes.shape, jnp.float32),
        compiler_params=pltpu.CompilerParams(vmem_limit_bytes=60 * 1024 * 1024),
        cost_estimate=pl.CostEstimate(flops=3 * 10**9, bytes_accessed=18 * 10**6, transcendentals=0),
    )(planes, wiener, velocity, gradient, below, above, wall_derivative)


def padded(values, rows, columns):
    return jnp.pad(
        values, ((0, rows - values.shape[0]), (0, columns - values.shape[1]))
    )


def stacked_three(table):
    table = np.asarray(table, np.float32)
    high = table.astype(jnp.bfloat16)
    low = (table - high.astype(np.float32)).astype(jnp.bfloat16)
    return jnp.asarray(np.concatenate([high, high, low], axis=0))


def split_three(table, axis):
    high = lax.reduce_precision(table, 8, 7)
    low = (table - high).astype(jnp.bfloat16)
    high = high.astype(jnp.bfloat16)
    return jnp.concatenate([high, high, low], axis=axis)


def three_of(values, axis):
    high = values.astype(jnp.bfloat16)
    low = (values - high.astype(jnp.float32)).astype(jnp.bfloat16)
    return jnp.concatenate([high, low, high], axis=axis)


def full_dot(a, b, side=0):
    return lax.dot_general(
        a,
        b,
        (((1,), (side,)), ((), ())),
        precision=FULL,
        preferred_element_type=jnp.float32,
    )


def plane_kernel(n_ref, s_ref, v_ref, m_ref, x_ref, o_ref, t_ref):
    k = pl.program_id(0)
    count = pl.num_programs(0)
    size_y, size_x = s_ref.shape

    @pl.when(k == 0)
    def _():
        t_ref[...] = jnp.zeros_like(t_ref)

    for start in range(0, size_y, 64):
        part = pl.ds(start, min(64, size_y - start))
        moved = [n_ref[0, c, part, :] for c in range(3)]
        for p, (i, j) in enumerate(PAIRS):
            t_ref[p, part, :] += moved[i] * moved[j]

    @pl.when(k == count - 1)
    def _():
        for start in range(0, size_y, 64):
            part = pl.ds(start, min(64, size_y - start))
            spring = s_ref[part, :]
            for p, (i, j) in enumerate(PAIRS):
                value = spring * (t_ref[p, part, :] / count)
                t_ref[p, part, :] = value - 1.0 if i == j else value
        scaled, slope = m_ref[:LANES, :], m_ref[LANES:, :]
        for i in range(3):
            column = [t_ref[p] for p in COLUMN[i]]
            direct = v_ref[i] + jnp.dot(
                slope, three_of(column[1], 0), preferred_element_type=jnp.float32
            )
            along = jnp.dot(
                scaled,
                three_of(jnp.concatenate([column[0], column[2]], axis=1), 0),
                preferred_element_type=jnp.float32,
            )
            force = full_dot(
                x_ref[...], jnp.concatenate([direct, along[:, :size_x]], axis=1), 1
            )
            force_z = full_dot(x_ref[:, :size_x], along[:, size_x:], 1)
            for half in range(2):
                lanes = slice(half * 128, half * 128 + 128)
                o_ref[pl.ds(8 * half + i, 128, stride=16), :] = force[:, lanes]
                o_ref[pl.ds(8 * half + 3 + i, 128, stride=16), :] = force_z[:, lanes]


def own_plane(moved, spring, modes_velocity, modes, rows):
    count, _, size_y, size_x = moved.shape
    whole = pl.BlockSpec(memory_space=pltpu.VMEM)
    message = pl.pallas_call(
        plane_kernel,
        grid=(count,),
        in_specs=[
            pl.BlockSpec((1, 3, size_y, size_x), lambda k: (k, 0, 0, 0)),
            whole,
            whole,
            whole,
            whole,
        ],
        out_specs=pl.BlockSpec((size_x * 16, 128), lambda k: (0, 0)),
        out_shape=jax.ShapeDtypeStruct((size_x * 16, 128), jnp.float32),
        scratch_shapes=[pltpu.VMEM((6, LANES, size_x), jnp.float32)],
        compiler_params=pltpu.CompilerParams(vmem_limit_bytes=24 * 1024 * 1024),
    )(moved, spring, modes_velocity, modes, rows)
    return message.reshape(size_x, 2, 8, 128)


def row_kernel(spans, in_ref, d_ref, f_ref, g_ref, b_ref, o_ref, t_ref, sem):
    flat = in_ref.reshape(in_ref.shape[0] * 16, 128)
    lane = lax.broadcasted_iota(jnp.int32, (128, 128), 1)
    last = jnp.zeros((128, 128), jnp.float32)

    def loaded(c):
        return jnp.concatenate(
            [flat[pl.ds(8 * half + c, 128, stride=16), :] for half in range(2)], axis=1
        )

    for i in range(3):
        solved = full_dot(f_ref[...], loaded(i)) + full_dot(g_ref[...], loaded(3 + i))
        both = full_dot(b_ref[...], solved / d_ref[...])
        value, slope = both[:128], both[128:]
        t_ref[:, i] = value[:, :128].reshape(spans, 8, 128)
        t_ref[:, 3 + i] = slope[:, :128].reshape(spans, 8, 128)
        value, slope = value[:, 128:], slope[:, 128:]
        mixed = jnp.where(lane < 64, value, pltpu.roll(slope, 64, 1))
        t_ref[:, 6 + i] = mixed.reshape(spans, 8, 128)
        last = jnp.where(lane == i, pltpu.roll(value, 64 + i, 1), last)
        last = jnp.where(lane == 3 + i, pltpu.roll(slope, 67 + i, 1), last)
    t_ref[:, 9] = last.reshape(spans, 8, 128)
    copies = [
        pltpu.make_async_copy(t_ref, o_ref.at[pl.ds(k * spans, spans)], sem.at[k])
        for k in range(o_ref.shape[0] // spans)
    ]
    for copy in copies:
        copy.start()
    for copy in copies:
        copy.wait()


def own_row(spectra, damping, forward, forward_slope, inverse, samples, spans):
    whole = pl.BlockSpec(memory_space=pltpu.VMEM)
    return pl.pallas_call(
        functools.partial(row_kernel, spans),
        in_specs=[whole] * 5,
        out_specs=pl.BlockSpec(memory_space=pltpu.HBM),
        out_shape=pltpu.HBM((samples * spans, 10, 8, 128), jnp.float32),
        scratch_shapes=[
            pltpu.VMEM((spans, 10, 8, 128), jnp.float32),
            pltpu.SemaphoreType.DMA((samples,)),
        ],
        compiler_params=pltpu.CompilerParams(vmem_limit_bytes=32 * 1024 * 1024),
    )(spectra, damping, forward, forward_slope, inverse)


def slab_kernel(u_ref, w_ref, h_ref, l_ref, t_ref, x_ref, v_ref, g_ref):
    i = pl.program_id(0)
    rows = u_ref.shape[0]
    _, size_y, slab, size_x = v_ref.shape
    flat = [r.reshape(rows * slab, 128) for r in (u_ref, w_ref, h_ref, l_ref)]
    out_v = v_ref.reshape(size_y * slab, size_x)
    out_g = g_ref.reshape(3, size_y * slab, size_x)
    lane = lax.broadcasted_iota(jnp.int32, (rows, 128), 1)
    half = t_ref.shape[0] // 2
    for first in range(0, slab, 2):
        values, slopes = [], []
        for z in (first, first + 1):
            value, slope, high, last = [r[pl.ds(z, rows, stride=slab), :] for r in flat]
            value_high = jnp.where(lane < 64, high, pltpu.roll(last, 64 - i, 1))
            slope_high = jnp.where(
                lane < 64, pltpu.roll(high, 64, 1), pltpu.roll(last, 61 - i, 1)
            )
            value_high = jnp.where(lane <= 64, value_high, 0.0)
            slope_high = jnp.where(lane <= 64, slope_high, 0.0)
            values.append(jnp.concatenate([value, value_high], axis=1))
            slopes.append(jnp.concatenate([slope, slope_high], axis=1))
        across = (((1,), (1,)), ((), ()))
        value = lax.dot_general(
            t_ref[...],
            three_of(jnp.concatenate(values, axis=0), 1),
            across,
            preferred_element_type=jnp.float32,
        )
        slope = lax.dot_general(
            t_ref[:half],
            three_of(jnp.concatenate(slopes, axis=0), 1),
            across,
            preferred_element_type=jnp.float32,
        )
        for k, z in enumerate((first, first + 1)):
            place = pl.ds(z, size_y, stride=slab)
            lanes = slice(k * rows, k * rows + rows)
            both = jnp.dot(
                three_of(value[:half, lanes], 1), x_ref[...], preferred_element_type=jnp.float32
            )
            out_v[place, :] = both[:size_y, :size_x]
            out_g[0, place, :] = both[:size_y, size_x:]
            both = jnp.dot(
                three_of(jnp.concatenate([value[half:, lanes], slope[:, lanes]], axis=0), 1),
                x_ref[:, :size_x],
                preferred_element_type=jnp.float32,
            )
            out_g[1, place, :] = both[:size_y]
            out_g[2, place, :] = both[half : half + size_y]


def slab_values(rows, wall_table, table_x, size_y):
    count = rows.shape[0]
    slab, size_x = rows.shape[2], table_x.shape[1] // 2
    whole = pl.BlockSpec(memory_space=pltpu.VMEM)

    def piece(place):
        return pl.BlockSpec((count, 1, slab, 128), lambda i: (0, place(i), 0, 0))

    return pl.pallas_call(
        slab_kernel,
        grid=(3,),
        in_specs=[
            piece(lambda i: i),
            piece(lambda i: i + 3),
            piece(lambda i: i + 6),
            piece(lambda i: 9),
            whole,
            whole,
        ],
        out_specs=(
            pl.BlockSpec((1, size_y, slab, size_x), lambda i: (i, 0, 0, 0)),
            pl.BlockSpec((3, size_y, slab, size_x), lambda i: (i, 0, 0, 0)),
        ),
        out_shape=(
            jax.ShapeDtypeStruct((3, size_y, slab, size_x), jnp.float32),
            jax.ShapeDtypeStruct((9, size_y, slab, size_x), jnp.float32),
        ),
        compiler_params=pltpu.CompilerParams(vmem_limit_bytes=60 * 1024 * 1024),
    )(rows, rows, rows, rows, wall_table, table_x)


def summed(planes):
    count = lax.axis_size("sample")
    ring = count // 2
    index = lax.axis_index("sample")
    place = index % ring
    quarters = planes.reshape((ring, planes.shape[0] // ring) + planes.shape[1:])

    def shifted(values, k):
        pairs = [(i, i - i % ring + (i + k) % ring) for i in range(count)]
        return lax.ppermute(values, "sample", pairs)

    ahead = lax.dynamic_slice_in_dim(
        jnp.concatenate([quarters, quarters]), place, ring, axis=0
    )
    total = ahead[0]
    for part in [shifted(ahead[k], k) for k in range(1, ring)]:
        total = total + part
    pairs = [(i, (i + ring) % count) for i in range(count)]
    total = total + lax.ppermute(total, "sample", pairs)
    parts = [shifted(total, k) for k in range(ring - 1, 0, -1)] + [total]
    start = (ring - 1 - place) % ring
    gathered = lax.dynamic_slice_in_dim(jnp.stack(parts + parts), start, ring, axis=0)
    return gathered.reshape(planes.shape)


def on_device(
    fields, wiener, velocity, gradient, wall_derivative, to_modes, from_modes, mode_rates
):
    size_x, slab, size_y = fields.shape[2:]
    samples = lax.axis_size("sample")
    spans = lax.axis_size("span")
    size_z = slab * spans
    step_x = LENGTH_X / size_x
    step_z = LENGTH_Z / size_z
    coupling = TIME_STEP * POLYMER_WEIGHT
    relax = TIME_STEP / (2.0 * WEISSENBERG)

    rows_x, slope_rows_x, square_x = real_basis(size_x, LENGTH_X)
    rows_z, slope_rows_z, square_z = real_basis(size_z, LENGTH_Z)
    order = np.array([slab * (d % spans) + d // spans for d in range(samples * spans)])

    field = jnp.transpose(fields[:, 0], (2, 0, 3, 1))
    ahead = [(i, (i + 1) % spans) for i in range(spans)]
    back = [((i + 1) % spans, i) for i in range(spans)]
    below = lax.ppermute(field[-1], "span", ahead)
    above = lax.ppermute(field[0], "span", back)
    total_square = summed(jnp.sum(field * field, axis=1))
    speed = jnp.transpose(velocity, (0, 3, 2, 1))
    free = spring_free(
        field,
        jnp.transpose(wiener[:, 0], (0, 3, 2, 1)),
        speed,
        jnp.transpose(gradient, (0, 3, 2, 1)),
        below,
        above,
        wall_derivative,
        step_x,
        step_z,
    )
    slab_spring = 1.0 / (1.0 - total_square / samples / EXTENSIBILITY)
    new_fields = free - relax * slab_spring[:, None] * field
    moved = lax.all_to_all(new_fields, "sample", 0, 0, tiled=True)

    own_velocity = lax.dynamic_index_in_dim(
        speed, lax.axis_index("sample"), 2, keepdims=False
    )
    modes = padded(to_modes, LANES, size_y)
    modes_slope = coupling * jnp.dot(modes, wall_derivative, precision=FULL)
    modes_velocity = jnp.einsum("my,cyx->cmx", modes, own_velocity, precision=FULL)
    modes_table = jnp.concatenate([coupling * modes, modes_slope])
    spring = lax.dynamic_index_in_dim(
        slab_spring, lax.axis_index("sample"), 0, keepdims=False
    )
    message = own_plane(
        moved,
        spring,
        modes_velocity,
        split_three(padded(modes_table, 2 * LANES, LANES), 1),
        f32(np.concatenate([rows_x, slope_rows_x @ rows_x], axis=1)),
    )
    spectra = lax.all_to_all(message, BOTH, 0, 0, tiled=True)

    row = lax.axis_index("sample") * spans + lax.axis_index("span")
    square_row = lax.dynamic_index_in_dim(f32(square_x), row, 0, keepdims=False)
    rates = padded(mode_rates[None, :], 1, LANES)
    damping = 1.0 + TIME_STEP * VISCOSITY * (
        square_row + f32(square_z)[:, None] + rates
    )
    back = own_row(
        spectra,
        damping,
        f32(rows_z[:, order]),
        f32((slope_rows_z @ rows_z)[:, order]),
        f32(np.concatenate([rows_z.T, rows_z.T @ slope_rows_z])),
        samples,
        spans,
    )
    rows = lax.all_to_all(back, BOTH, 0, 0, tiled=True)

    modes_wall = jnp.dot(wall_derivative, from_modes, precision=FULL)
    wall_table = jnp.concatenate(
        [padded(from_modes, 208, LANES), padded(modes_wall, 208, LANES)]
    )
    new_velocity, new_gradient = slab_values(
        rows,
        split_three(wall_table, 1),
        stacked_three(np.concatenate([rows_x, (rows_x.T @ slope_rows_x).T], axis=1)),
        size_y,
    )
    return (
        jnp.transpose(new_fields, (1, 3, 0, 2))[:, None],
        jnp.transpose(new_velocity, (0, 3, 2, 1)),
        jnp.transpose(new_gradient, (0, 3, 2, 1)),
    )


def solution(mesh):
    in_specs = (
        P(None, "sample", None, "span", None),
        P(None, "sample", None, "span", None),
        P(None, None, "span", None),
        P(None, None, "span", None),
        P(),
        P(),
        P(),
        P(),
    )
    out_specs = (
        P(None, "sample", None, "span", None),
        P(None, None, "span", None),
        P(None, None, "span", None),
    )
    return jax.shard_map(
        on_device, mesh=mesh, in_specs=in_specs, out_specs=out_specs, check_vma=False
    )
```

```python
import functools
import math

import jax
import jax.numpy as jnp
import numpy as np
from jax import lax
from jax.experimental import pallas as pl
from jax.experimental.pallas import tpu as pltpu
from jax.sharding import PartitionSpec as P

TIME_STEP = 0.01
WEISSENBERG = 0.05
EXTENSIBILITY = 10.0
POLYMER_WEIGHT = 5.0
VISCOSITY = 0.5
DIFFUSIVITY = 0.003
LENGTH_X = math.pi
LENGTH_Z = 2.0 * math.pi / 3.0
FULL = lax.Precision.HIGHEST
HIGH = lax.Precision.HIGH
BOTH = ("sample", "span")
LANES = 256
PAIRS = ((0, 0), (0, 1), (0, 2), (1, 1), (1, 2), (2, 2))
COLUMN = ((0, 1, 2), (1, 3, 4), (2, 4, 5))


def real_basis(count, extent):
    half = count // 2
    place = np.arange(count)
    rows = np.zeros((count, count))
    kappa = np.zeros(count)
    slope = np.zeros((count, count))
    unit = 2.0 * math.pi / extent
    rows[0] = math.sqrt(1.0 / count)
    for k in range(1, half):
        angle = 2.0 * math.pi * ((k * place) % count) / count
        rows[k] = math.sqrt(2.0 / count) * np.cos(angle)
        rows[half + k] = math.sqrt(2.0 / count) * np.sin(angle)
        kappa[k] = kappa[half + k] = unit * k
        slope[k, half + k] = unit * k
        slope[half + k, k] = -unit * k
    rows[half] = math.sqrt(1.0 / count) * (1.0 - 2.0 * (place % 2))
    kappa[half] = unit * half
    return rows, slope, kappa * kappa


def f32(values):
    return jnp.asarray(np.asarray(values, np.float32))


def free_kernel(scales, f_ref, w_ref, v_ref, g_ref, lo_ref, hi_ref, d_ref, e_ref, o_ref):
    scale_x, scale_z, scale_c, scale_w = scales
    i = pl.program_id(0)
    slab, _, size_y, size_x = f_ref.shape
    noise, speed, tensor = [
        r.reshape(r.shape[0], size_y * slab, size_x) for r in (w_ref, v_ref, g_ref)
    ]
    slopes = []
    for z in range(slab):
        plane = pl.ds(z, size_y, stride=slab)
        own = f_ref[z, i]
        if z % 2 == 0:
            pair = jnp.concatenate([own, f_ref[z + 1, i]], axis=1)
            high = pair.astype(jnp.bfloat16)
            low = (pair - high.astype(jnp.float32)).astype(jnp.bfloat16)
            slope = jnp.dot(d_ref[...], high, preferred_element_type=jnp.float32)
            slope += jnp.dot(d_ref[...], low, preferred_element_type=jnp.float32)
            slope += jnp.dot(e_ref[...], high, preferred_element_type=jnp.float32)
            slopes = [slope[:, :size_x], slope[:, size_x:]]
        slope_y = slopes[z % 2]
        upper = hi_ref[i] if z == slab - 1 else f_ref[z + 1, i]
        lower = lo_ref[i] if z == 0 else f_ref[z - 1, i]
        slope_x = pltpu.roll(own, size_x - 1, 1) - pltpu.roll(own, 1, 1)
        advect = (
            speed[0, plane, :] * (scale_x * slope_x)
            + speed[1, plane, :] * slope_y
            + speed[2, plane, :] * (scale_z * (upper - lower))
        )
        stretch = (
            tensor[0, plane, :] * f_ref[z, 0]
            + tensor[1, plane, :] * f_ref[z, 1]
            + tensor[2, plane, :] * f_ref[z, 2]
        )
        result = own + TIME_STEP * (stretch - advect)
        result = result + scale_c * (upper - 2.0 * own + lower)
        o_ref[z, 0] = result + scale_w * noise[0, plane, :]


def spring_free(planes, wiener, velocity, gradient, below, above, wall_derivative, step_x, step_z):
    slab, _, size_y, size_x = planes.shape
    whole = pl.BlockSpec(memory_space=pltpu.VMEM)
    high = lax.reduce_precision(wall_derivative, 8, 7)
    low = (wall_derivative - high).astype(jnp.bfloat16)
    high = high.astype(jnp.bfloat16)
    scales = (
        1.0 / (2.0 * step_x),
        1.0 / (2.0 * step_z),
        DIFFUSIVITY * TIME_STEP / (step_z * step_z),
        math.sqrt(TIME_STEP / WEISSENBERG),
    )
    return pl.pallas_call(
        functools.partial(free_kernel, scales),
        grid=(3,),
        in_specs=[
            whole,
            pl.BlockSpec((1, size_y, slab, size_x), lambda i: (i, 0, 0, 0)),
            whole,
            pl.BlockSpec((3, size_y, slab, size_x), lambda i: (i, 0, 0, 0)),
            whole,
            whole,
            whole,
            whole,
        ],
        out_specs=pl.BlockSpec((slab, 1, size_y, size_x), lambda i: (0, i, 0, 0)),
        out_shape=pltpu.HBM(planes.shape, jnp.float32),
        compiler_params=pltpu.CompilerParams(vmem_limit_bytes=60 * 1024 * 1024),
        cost_estimate=pl.CostEstimate(flops=3 * 10**9, bytes_accessed=18 * 10**6, transcendentals=0),
    )(planes, wiener, velocity, gradient, below, above, high, low)


def padded(values, rows, columns):
    return jnp.pad(
        values, ((0, rows - values.shape[0]), (0, columns - values.shape[1]))
    )


def stacked_three(table):
    table = np.asarray(table, np.float32)
    high = table.astype(jnp.bfloat16)
    low = (table - high.astype(np.float32)).astype(jnp.bfloat16)
    return jnp.asarray(np.concatenate([high, high, low], axis=0))


def split_three(table, axis):
    high = lax.reduce_precision(table, 8, 7)
    low = (table - high).astype(jnp.bfloat16)
    high = high.astype(jnp.bfloat16)
    return jnp.concatenate([high, high, low], axis=axis)


def three_of(values, axis):
    high = values.astype(jnp.bfloat16)
    low = (values - high.astype(jnp.float32)).astype(jnp.bfloat16)
    return jnp.concatenate([high, low, high], axis=axis)


def full_dot(a, b, side=0):
    return lax.dot_general(
        a,
        b,
        (((1,), (side,)), ((), ())),
        precision=FULL,
        preferred_element_type=jnp.float32,
    )


def plane_kernel(n_ref, s_ref, v_ref, m_ref, x_ref, o_ref, t_ref):
    k = pl.program_id(0)
    count = pl.num_programs(0)
    size_y, size_x = s_ref.shape

    @pl.when(k == 0)
    def _():
        t_ref[...] = jnp.zeros_like(t_ref)

    for start in range(0, size_y, 64):
        part = pl.ds(start, min(64, size_y - start))
        moved = [n_ref[0, c, part, :] for c in range(3)]
        for p, (i, j) in enumerate(PAIRS):
            t_ref[p, part, :] += moved[i] * moved[j]

    @pl.when(k == count - 1)
    def _():
        for start in range(0, size_y, 64):
            part = pl.ds(start, min(64, size_y - start))
            spring = s_ref[part, :]
            for p, (i, j) in enumerate(PAIRS):
                value = spring * (t_ref[p, part, :] / count)
                t_ref[p, part, :] = value - 1.0 if i == j else value
        scaled, slope = m_ref[:LANES, :], m_ref[LANES:, :]
        last_mode = size_y - 1
        rest = [None] * 6
        for i in range(3):
            column = [t_ref[p] for p in COLUMN[i]]
            direct = v_ref[i] + jnp.dot(
                slope, three_of(column[1], 0), preferred_element_type=jnp.float32
            )
            along = jnp.dot(
                scaled,
                three_of(jnp.concatenate([column[0], column[2]], axis=1), 0),
                preferred_element_type=jnp.float32,
            )
            force = full_dot(
                x_ref[...], jnp.concatenate([direct, along[:, :size_x]], axis=1), 1
            )
            force_z = full_dot(x_ref[:, :size_x], along[:, size_x:], 1)
            top = slice(last_mode, last_mode + 8)
            own = jnp.concatenate([direct[top], along[top, :size_x]], axis=1)
            rest[i] = full_dot(own, x_ref[...], 1)[:1]
            rest[3 + i] = full_dot(along[top, size_x:], x_ref[:, :size_x], 1)[:1]
            for half in range(2):
                lanes = slice(half * 128, half * 128 + 128)
                o_ref[pl.ds(8 * half + i, 128, stride=16), :] = force[:, lanes]
                o_ref[pl.ds(8 * half + 3 + i, 128, stride=16), :] = force_z[:, lanes]
        lane = lax.broadcasted_iota(jnp.int32, (128, 128), 1)
        for c in range(2):
            o_ref[pl.ds(6 + c, 128, stride=16), :] = jnp.broadcast_to(rest[c], (128, 128))
        for c in range(4):
            for part in range(2):
                row = jnp.broadcast_to(rest[2 + c], (128, 128))
                row = row if part else pltpu.roll(row, 64, 1)
                place = pl.ds(8 + 2 * c + part, 128, stride=16)
                kept = o_ref[place, :] if 2 * c + part < 6 else jnp.zeros_like(row)
                o_ref[place, :] = jnp.where(lane < 64, kept, row)


def own_plane(moved, spring, modes_velocity, modes, rows):
    count, _, size_y, size_x = moved.shape
    whole = pl.BlockSpec(memory_space=pltpu.VMEM)
    message = pl.pallas_call(
        plane_kernel,
        grid=(count,),
        in_specs=[
            pl.BlockSpec((1, 3, size_y, size_x), lambda k: (k, 0, 0, 0)),
            whole,
            whole,
            whole,
            whole,
        ],
        out_specs=pl.BlockSpec((size_x * 16, 128), lambda k: (0, 0)),
        out_shape=jax.ShapeDtypeStruct((size_x * 16, 128), jnp.float32),
        scratch_shapes=[pltpu.VMEM((6, LANES, size_x), jnp.float32)],
        compiler_params=pltpu.CompilerParams(vmem_limit_bytes=24 * 1024 * 1024),
    )(moved, spring, modes_velocity, modes, rows)
    return message.reshape(size_x, 2, 8, 128)


def row_kernel(spans, in_ref, d_ref, e_ref, f_ref, g_ref, b_ref, w_ref, o_ref, l_ref, t_ref, sem):
    flat = in_ref.reshape(in_ref.shape[0] * 16, 128)
    lane = lax.broadcasted_iota(jnp.int32, (128, 128), 1)

    def taken(c):
        return flat[pl.ds(c, 128, stride=16), :]

    def loaded(c):
        return jnp.concatenate([taken(c), taken(8 + c)], axis=1)

    for i in range(3):
        solved = full_dot(f_ref[...], loaded(i)) + full_dot(g_ref[...], loaded(3 + i))
        both = full_dot(b_ref[...], solved / d_ref[...])
        value, slope = both[:128], both[128:]
        t_ref[:, i] = value[:, :128].reshape(spans, 8, 128)
        t_ref[:, 3 + i] = slope[:, :128].reshape(spans, 8, 128)
        mixed = jnp.where(lane < 64, value[:, 128:], pltpu.roll(slope[:, 128:], 64, 1))
        t_ref[:, 6 + i] = mixed.reshape(spans, 8, 128)
    copies = [
        pltpu.make_async_copy(t_ref, o_ref.at[pl.ds(k * spans, spans)], sem.at[k])
        for k in range(o_ref.shape[0] // spans)
    ]
    for copy in copies:
        copy.start()

    def last(c):
        if c < 2:
            return taken(6 + c)
        first, second = taken(8 + 2 * (c - 2)), taken(9 + 2 * (c - 2))
        return jnp.where(lane < 64, pltpu.roll(first, 64, 1), second)

    for i in range(3):
        solved = full_dot(f_ref[...], last(i)) + full_dot(g_ref[...], last(3 + i))
        both = full_dot(w_ref[...], solved / e_ref[...])
        l_ref[i] = both[:8]
        l_ref[3 + i] = both[8:]
    for copy in copies:
        copy.wait()


def own_row(spectra, damping, last_damping, forward, forward_slope, inverse, slab_inverse, samples, spans):
    whole = pl.BlockSpec(memory_space=pltpu.VMEM)
    return pl.pallas_call(
        functools.partial(row_kernel, spans),
        in_specs=[whole] * 7,
        out_specs=(pl.BlockSpec(memory_space=pltpu.HBM), whole),
        out_shape=(
            pltpu.HBM((samples * spans, 9, 8, 128), jnp.float32),
            jax.ShapeDtypeStruct((6, 8, 128), jnp.float32),
        ),
        scratch_shapes=[
            pltpu.VMEM((spans, 9, 8, 128), jnp.float32),
            pltpu.SemaphoreType.DMA((samples,)),
        ],
        compiler_params=pltpu.CompilerParams(vmem_limit_bytes=32 * 1024 * 1024),
    )(spectra, damping, last_damping, forward, forward_slope, inverse, slab_inverse)


def slab_kernel(u_ref, w_ref, h_ref, l_ref, t_ref, c_ref, x_ref, v_ref, g_ref):
    i = pl.program_id(0)
    rows = u_ref.shape[0]
    _, size_y, slab, size_x = v_ref.shape
    flat = [r.reshape(rows * slab, 128) for r in (u_ref, w_ref, h_ref)]
    out_v = v_ref.reshape(size_y * slab, size_x)
    out_g = g_ref.reshape(3, size_y * slab, size_x)
    lane = lax.broadcasted_iota(jnp.int32, (rows, 128), 1)
    half = t_ref.shape[0] // 2
    for first in range(0, slab, 2):
        values, slopes = [], []
        for z in (first, first + 1):
            value, slope, high = [r[pl.ds(z, rows, stride=slab), :] for r in flat]
            value_high = jnp.where(lane < 64, high, 0.0)
            slope_high = jnp.where(lane < 64, pltpu.roll(high, 64, 1), 0.0)
            values.append(jnp.concatenate([value, value_high], axis=1))
            slopes.append(jnp.concatenate([slope, slope_high], axis=1))
        across = (((1,), (1,)), ((), ()))
        value = lax.dot_general(
            t_ref[...],
            three_of(jnp.concatenate(values, axis=0), 1),
            across,
            preferred_element_type=jnp.float32,
        )
        slope = lax.dot_general(
            t_ref[:half],
            three_of(jnp.concatenate(slopes, axis=0), 1),
            across,
            preferred_element_type=jnp.float32,
        )
        for k, z in enumerate((first, first + 1)):
            place = pl.ds(z, size_y, stride=slab)
            lanes = slice(k * rows, k * rows + rows)
            value_z = value[:, lanes] + c_ref[...] * l_ref[i, pl.ds(z, 1), :]
            slope_z = slope[:, lanes] + c_ref[:half] * l_ref[3 + i, pl.ds(z, 1), :]
            both = jnp.dot(
                three_of(value_z[:half], 1), x_ref[...], preferred_element_type=jnp.float32
            )
            out_v[place, :] = both[:size_y, :size_x]
            out_g[0, place, :] = both[:size_y, size_x:]
            both = jnp.dot(
                three_of(jnp.concatenate([value_z[half:], slope_z], axis=0), 1),
                x_ref[:, :size_x],
                preferred_element_type=jnp.float32,
            )
            out_g[1, place, :] = both[:size_y]
            out_g[2, place, :] = both[half : half + size_y]


def slab_values(rows, last, wall_table, last_column, table_x, size_y):
    count = rows.shape[0]
    slab, size_x = rows.shape[2], table_x.shape[1] // 2
    whole = pl.BlockSpec(memory_space=pltpu.VMEM)

    def piece(place):
        return pl.BlockSpec((count, 1, slab, 128), lambda i: (0, place(i), 0, 0))

    return pl.pallas_call(
        slab_kernel,
        grid=(3,),
        in_specs=[
            piece(lambda i: i),
            piece(lambda i: i + 3),
            piece(lambda i: i + 6),
            whole,
            whole,
            whole,
            whole,
        ],
        out_specs=(
            pl.BlockSpec((1, size_y, slab, size_x), lambda i: (i, 0, 0, 0)),
            pl.BlockSpec((3, size_y, slab, size_x), lambda i: (i, 0, 0, 0)),
        ),
        out_shape=(
            jax.ShapeDtypeStruct((3, size_y, slab, size_x), jnp.float32),
            jax.ShapeDtypeStruct((9, size_y, slab, size_x), jnp.float32),
        ),
        compiler_params=pltpu.CompilerParams(vmem_limit_bytes=60 * 1024 * 1024),
    )(rows, rows, rows, last, wall_table, last_column, table_x)


def summed(planes, beside):
    count = lax.axis_size("sample")
    ring = count // 2
    index = lax.axis_index("sample")
    place = index % ring
    quarters = planes.reshape((ring, planes.shape[0] // ring) + planes.shape[1:])

    def shifted(values, k):
        pairs = [(i, i - i % ring + (i + k) % ring) for i in range(count)]
        return lax.ppermute(values, "sample", pairs)

    ahead = lax.dynamic_slice_in_dim(
        jnp.concatenate([quarters, quarters]), place, ring, axis=0
    )
    total = ahead[0]
    for part in [shifted(ahead[k], k) for k in range(1, ring)]:
        total = total + part
    pairs = [(i, (i + ring) % count) for i in range(count)]
    total = total + lax.ppermute(total, "sample", pairs)
    total, beside = lax.optimization_barrier((total, beside))
    parts = [shifted(total, k) for k in range(ring - 1, 0, -1)] + [total]
    start = (ring - 1 - place) % ring
    gathered = lax.dynamic_slice_in_dim(jnp.stack(parts + parts), start, ring, axis=0)
    return gathered.reshape(planes.shape), beside


def on_device(
    fields, wiener, velocity, gradient, wall_derivative, to_modes, from_modes, mode_rates
):
    size_x, slab, size_y = fields.shape[2:]
    samples = lax.axis_size("sample")
    spans = lax.axis_size("span")
    size_z = slab * spans
    step_x = LENGTH_X / size_x
    step_z = LENGTH_Z / size_z
    coupling = TIME_STEP * POLYMER_WEIGHT
    relax = TIME_STEP / (2.0 * WEISSENBERG)

    rows_x, slope_rows_x, square_x = real_basis(size_x, LENGTH_X)
    rows_z, slope_rows_z, square_z = real_basis(size_z, LENGTH_Z)
    order = np.array([slab * (d % spans) + d // spans for d in range(samples * spans)])

    field = jnp.transpose(fields[:, 0], (2, 0, 3, 1))
    ahead = [(i, (i + 1) % spans) for i in range(spans)]
    back = [((i + 1) % spans, i) for i in range(spans)]
    below = lax.ppermute(field[-1], "span", ahead)
    above = lax.ppermute(field[0], "span", back)
    speed = jnp.transpose(velocity, (0, 3, 2, 1))
    free = spring_free(
        field,
        jnp.transpose(wiener[:, 0], (0, 3, 2, 1)),
        speed,
        jnp.transpose(gradient, (0, 3, 2, 1)),
        below,
        above,
        wall_derivative,
        step_x,
        step_z,
    )
    total_square, free = summed(jnp.sum(field * field, axis=1), free)
    slab_spring = 1.0 / (1.0 - total_square / samples / EXTENSIBILITY)
    new_fields = free - relax * slab_spring[:, None] * field
    moved = lax.all_to_all(new_fields, "sample", 0, 0, tiled=True)

    own_velocity = lax.dynamic_index_in_dim(
        speed, lax.axis_index("sample"), 2, keepdims=False
    )
    modes = padded(to_modes, LANES, size_y)
    modes_slope = coupling * jnp.dot(modes, wall_derivative, precision=FULL)
    modes_velocity = jnp.einsum("my,cyx->cmx", modes, own_velocity, precision=FULL)
    modes_table = jnp.concatenate([coupling * modes, modes_slope])
    spring = lax.dynamic_index_in_dim(
        slab_spring, lax.axis_index("sample"), 0, keepdims=False
    )
    message = own_plane(
        moved,
        spring,
        modes_velocity,
        split_three(padded(modes_table, 2 * LANES, LANES), 1),
        f32(np.concatenate([rows_x, slope_rows_x @ rows_x], axis=1)),
    )
    spectra = lax.all_to_all(message, BOTH, 0, 0, tiled=True)

    row = lax.axis_index("sample") * spans + lax.axis_index("span")
    square_row = lax.dynamic_index_in_dim(f32(square_x), row, 0, keepdims=False)
    rates = padded(mode_rates[None, :], 1, LANES)
    damping = 1.0 + TIME_STEP * VISCOSITY * (
        square_row + f32(square_z)[:, None] + rates
    )
    last_damping = 1.0 + TIME_STEP * VISCOSITY * (
        f32(square_x)[None, :] + f32(square_z)[:, None] + mode_rates[size_y - 1]
    )
    inverse = np.stack([rows_z.T, rows_z.T @ slope_rows_z])
    slab_inverse = lax.dynamic_index_in_dim(
        f32(inverse.reshape(2, spans, slab, size_z)), lax.axis_index("span"), 1, keepdims=False
    ).reshape(2 * slab, size_z)
    back, last = own_row(
        spectra,
        damping,
        last_damping,
        f32(rows_z[:, order]),
        f32((slope_rows_z @ rows_z)[:, order]),
        f32(inverse.reshape(2 * size_z, size_z)),
        slab_inverse,
        samples,
        spans,
    )
    rows = lax.all_to_all(back, BOTH, 0, 0, tiled=True)

    modes_wall = jnp.dot(wall_derivative, from_modes, precision=FULL)
    wall_table = jnp.concatenate(
        [padded(from_modes, 208, LANES), padded(modes_wall, 208, LANES)]
    )
    new_velocity, new_gradient = slab_values(
        rows,
        last,
        split_three(wall_table.at[:, size_y - 1].set(0.0), 1),
        jnp.broadcast_to(wall_table[:, size_y - 1 : size_y], (wall_table.shape[0], 128)),
        stacked_three(np.concatenate([rows_x, (rows_x.T @ slope_rows_x).T], axis=1)),
        size_y,
    )
    return (
        jnp.transpose(new_fields, (1, 3, 0, 2))[:, None],
        jnp.transpose(new_velocity, (0, 3, 2, 1)),
        jnp.transpose(new_gradient, (0, 3, 2, 1)),
    )


def solution(mesh):
    in_specs = (
        P(None, "sample", None, "span", None),
        P(None, "sample", None, "span", None),
        P(None, None, "span", None),
        P(None, None, "span", None),
        P(),
        P(),
        P(),
        P(),
    )
    out_specs = (
        P(None, "sample", None, "span", None),
        P(None, None, "span", None),
        P(None, None, "span", None),
    )
    return jax.shard_map(
        on_device, mesh=mesh, in_specs=in_specs, out_specs=out_specs, check_vma=False
    )
```

```python
import functools
import math

import jax
import jax.numpy as jnp
import numpy as np
from jax import lax
from jax.experimental import pallas as pl
from jax.experimental.pallas import tpu as pltpu
from jax.sharding import PartitionSpec as P

TIME_STEP = 0.01
WEISSENBERG = 0.05
EXTENSIBILITY = 10.0
POLYMER_WEIGHT = 5.0
VISCOSITY = 0.5
DIFFUSIVITY = 0.003
LENGTH_X = math.pi
LENGTH_Z = 2.0 * math.pi / 3.0
FULL = lax.Precision.HIGHEST
HIGH = lax.Precision.HIGH
BOTH = ("sample", "span")
LANES = 256
PAIRS = ((0, 0), (0, 1), (0, 2), (1, 1), (1, 2), (2, 2))
COLUMN = ((0, 1, 2), (1, 3, 4), (2, 4, 5))


def real_basis(count, extent):
    half = count // 2
    place = np.arange(count)
    rows = np.zeros((count, count))
    kappa = np.zeros(count)
    slope = np.zeros((count, count))
    unit = 2.0 * math.pi / extent
    rows[0] = math.sqrt(1.0 / count)
    for k in range(1, half):
        angle = 2.0 * math.pi * ((k * place) % count) / count
        rows[k] = math.sqrt(2.0 / count) * np.cos(angle)
        rows[half + k] = math.sqrt(2.0 / count) * np.sin(angle)
        kappa[k] = kappa[half + k] = unit * k
        slope[k, half + k] = unit * k
        slope[half + k, k] = -unit * k
    rows[half] = math.sqrt(1.0 / count) * (1.0 - 2.0 * (place % 2))
    kappa[half] = unit * half
    return rows, slope, kappa * kappa


def f32(values):
    return jnp.asarray(np.asarray(values, np.float32))


def free_kernel(
    scales, f_ref, p_ref, w_ref, v_ref, g_ref, lo_ref, hi_ref, d_ref, e_ref, o_ref, s_ref
):
    scale_x, scale_z, scale_c, scale_w = scales
    slab, _, size_y, size_x = f_ref.shape
    block = p_ref.shape[2]
    here = pl.ds(pl.multiple_of(pl.program_id(0) * block, 8), block)

    @pl.when(pl.program_id(0) == 0)
    def _():
        for i in range(3):
            for z in range(0, slab, 2):
                pair = jnp.concatenate([f_ref[z, i], f_ref[z + 1, i]], axis=1)
                high = pair.astype(jnp.bfloat16)
                low = (pair - high.astype(jnp.float32)).astype(jnp.bfloat16)
                slope = jnp.dot(d_ref[...], high, preferred_element_type=jnp.float32)
                slope += jnp.dot(d_ref[...], low, preferred_element_type=jnp.float32)
                slope += jnp.dot(e_ref[...], high, preferred_element_type=jnp.float32)
                s_ref[z, i, :size_y, :] = slope[:, :size_x]
                s_ref[z + 1, i, :size_y, :] = slope[:, size_x:]

    noise, speed, tensor = [
        r.reshape(r.shape[0], block * slab, size_x) for r in (w_ref, v_ref, g_ref)
    ]
    for z in range(slab):
        plane = pl.ds(z, block, stride=slab)
        speed_x, speed_y, speed_z = [speed[c, plane, :] for c in range(3)]
        parts = [p_ref[z, c] for c in range(3)]
        for i in range(3):
            own = parts[i]
            upper = hi_ref[i] if z == slab - 1 else p_ref[z + 1, i]
            lower = lo_ref[i] if z == 0 else p_ref[z - 1, i]
            slope_x = pltpu.roll(own, size_x - 1, 1) - pltpu.roll(own, 1, 1)
            advect = (
                speed_x * (scale_x * slope_x)
                + speed_y * s_ref[z, i, here, :]
                + speed_z * (scale_z * (upper - lower))
            )
            stretch = (
                tensor[3 * i, plane, :] * parts[0]
                + tensor[3 * i + 1, plane, :] * parts[1]
                + tensor[3 * i + 2, plane, :] * parts[2]
            )
            result = own + TIME_STEP * (stretch - advect)
            result = result + scale_c * (upper - 2.0 * own + lower)
            o_ref[z, i] = result + scale_w * noise[i, plane, :]


def spring_free(planes, wiener, velocity, gradient, below, above, wall_derivative, step_x, step_z):
    slab, _, size_y, size_x = planes.shape
    block = 40
    steps = -(-size_y // block)
    whole = pl.BlockSpec(memory_space=pltpu.VMEM)
    high = lax.reduce_precision(wall_derivative, 8, 7)
    low = (wall_derivative - high).astype(jnp.bfloat16)
    high = high.astype(jnp.bfloat16)
    scales = (
        1.0 / (2.0 * step_x),
        1.0 / (2.0 * step_z),
        DIFFUSIVITY * TIME_STEP / (step_z * step_z),
        math.sqrt(TIME_STEP / WEISSENBERG),
    )

    def rows(count):
        return pl.BlockSpec((count, block, slab, size_x), lambda j: (0, j, 0, 0))

    across = pl.BlockSpec((slab, 3, block, size_x), lambda j: (0, 0, j, 0))
    edge = pl.BlockSpec((3, block, size_x), lambda j: (0, j, 0))
    return pl.pallas_call(
        functools.partial(free_kernel, scales),
        grid=(steps,),
        in_specs=[whole, across, rows(3), rows(3), rows(9), edge, edge, whole, whole],
        out_specs=across,
        out_shape=pltpu.HBM(planes.shape, jnp.float32),
        scratch_shapes=[pltpu.VMEM((slab, 3, steps * block, size_x), jnp.float32)],
        compiler_params=pltpu.CompilerParams(vmem_limit_bytes=60 * 1024 * 1024),
        cost_estimate=pl.CostEstimate(flops=3 * 10**9, bytes_accessed=18 * 10**6, transcendentals=0),
    )(planes, planes, wiener, velocity, gradient, below, above, high, low)


def padded(values, rows, columns):
    return jnp.pad(
        values, ((0, rows - values.shape[0]), (0, columns - values.shape[1]))
    )


def stacked_three(table):
    table = np.asarray(table, np.float32)
    high = table.astype(jnp.bfloat16)
    low = (table - high.astype(np.float32)).astype(jnp.bfloat16)
    return jnp.asarray(np.concatenate([high, high, low], axis=0))


def split_three(table, axis):
    high = lax.reduce_precision(table, 8, 7)
    low = (table - high).astype(jnp.bfloat16)
    high = high.astype(jnp.bfloat16)
    return jnp.concatenate([high, high, low], axis=axis)


def three_of(values, axis):
    high = values.astype(jnp.bfloat16)
    low = (values - high.astype(jnp.float32)).astype(jnp.bfloat16)
    return jnp.concatenate([high, low, high], axis=axis)


def full_dot(a, b, side=0):
    return lax.dot_general(
        a,
        b,
        (((1,), (side,)), ((), ())),
        precision=FULL,
        preferred_element_type=jnp.float32,
    )


def plane_kernel(n_ref, s_ref, v_ref, m_ref, x_ref, o_ref, t_ref):
    k = pl.program_id(0)
    count = pl.num_programs(0)
    size_y, size_x = s_ref.shape

    @pl.when(k == 0)
    def _():
        t_ref[...] = jnp.zeros_like(t_ref)

    for start in range(0, size_y, 64):
        part = pl.ds(start, min(64, size_y - start))
        moved = [n_ref[0, c, part, :] for c in range(3)]
        for p, (i, j) in enumerate(PAIRS):
            t_ref[p, part, :] += moved[i] * moved[j]

    @pl.when(k == count - 1)
    def _():
        for start in range(0, size_y, 64):
            part = pl.ds(start, min(64, size_y - start))
            spring = s_ref[part, :]
            for p, (i, j) in enumerate(PAIRS):
                value = spring * (t_ref[p, part, :] / count)
                t_ref[p, part, :] = value - 1.0 if i == j else value
        scaled, slope = m_ref[:LANES, :], m_ref[LANES:, :]
        last_mode = size_y - 1
        rest = [None] * 6
        for i in range(3):
            column = [t_ref[p] for p in COLUMN[i]]
            direct = v_ref[i] + jnp.dot(
                slope, three_of(column[1], 0), preferred_element_type=jnp.float32
            )
            along = jnp.dot(
                scaled,
                three_of(jnp.concatenate([column[0], column[2]], axis=1), 0),
                preferred_element_type=jnp.float32,
            )
            force = full_dot(
                x_ref[...], jnp.concatenate([direct, along[:, :size_x]], axis=1), 1
            )
            force_z = full_dot(x_ref[:, :size_x], along[:, size_x:], 1)
            top = slice(last_mode, last_mode + 8)
            own = jnp.concatenate([direct[top], along[top, :size_x]], axis=1)
            rest[i] = full_dot(own, x_ref[...], 1)[:1]
            rest[3 + i] = full_dot(along[top, size_x:], x_ref[:, :size_x], 1)[:1]
            for half in range(2):
                lanes = slice(half * 128, half * 128 + 128)
                o_ref[pl.ds(8 * half + i, 128, stride=16), :] = force[:, lanes]
                o_ref[pl.ds(8 * half + 3 + i, 128, stride=16), :] = force_z[:, lanes]
        lane = lax.broadcasted_iota(jnp.int32, (128, 128), 1)
        for c in range(2):
            o_ref[pl.ds(6 + c, 128, stride=16), :] = jnp.broadcast_to(rest[c], (128, 128))
        for c in range(4):
            for part in range(2):
                row = jnp.broadcast_to(rest[2 + c], (128, 128))
                row = row if part else pltpu.roll(row, 64, 1)
                place = pl.ds(8 + 2 * c + part, 128, stride=16)
                kept = o_ref[place, :] if 2 * c + part < 6 else jnp.zeros_like(row)
                o_ref[place, :] = jnp.where(lane < 64, kept, row)


def own_plane(moved, spring, modes_velocity, modes, rows):
    count, _, size_y, size_x = moved.shape
    whole = pl.BlockSpec(memory_space=pltpu.VMEM)
    message = pl.pallas_call(
        plane_kernel,
        grid=(count,),
        in_specs=[
            pl.BlockSpec((1, 3, size_y, size_x), lambda k: (k, 0, 0, 0)),
            whole,
            whole,
            whole,
            whole,
        ],
        out_specs=pl.BlockSpec((size_x * 16, 128), lambda k: (0, 0)),
        out_shape=jax.ShapeDtypeStruct((size_x * 16, 128), jnp.float32),
        scratch_shapes=[pltpu.VMEM((6, LANES, size_x), jnp.float32)],
        compiler_params=pltpu.CompilerParams(vmem_limit_bytes=24 * 1024 * 1024),
    )(moved, spring, modes_velocity, modes, rows)
    return message.reshape(size_x, 2, 8, 128)


def row_kernel(spans, in_ref, d_ref, e_ref, f_ref, g_ref, b_ref, w_ref, o_ref, l_ref, t_ref, sem):
    flat = in_ref.reshape(in_ref.shape[0] * 16, 128)
    lane = lax.broadcasted_iota(jnp.int32, (128, 128), 1)

    def taken(c):
        return flat[pl.ds(c, 128, stride=16), :]

    def loaded(c):
        return jnp.concatenate([taken(c), taken(8 + c)], axis=1)

    samples = o_ref.shape[0] // spans
    copies = []
    for i in range(3):
        solved = full_dot(f_ref[...], loaded(i)) + full_dot(g_ref[...], loaded(3 + i))
        both = full_dot(b_ref[...], solved / d_ref[...])
        value, slope = both[:128], both[128:]
        t_ref[i, :, 0] = value[:, :128].reshape(spans, 8, 128)
        t_ref[i, :, 1] = slope[:, :128].reshape(spans, 8, 128)
        mixed = jnp.where(lane < 64, value[:, 128:], pltpu.roll(slope[:, 128:], 64, 1))
        t_ref[i, :, 2] = mixed.reshape(spans, 8, 128)
        for k in range(samples):
            copy = pltpu.make_async_copy(
                t_ref.at[i], o_ref.at[pl.ds(k * spans, spans), i], sem.at[i, k]
            )
            copy.start()
            copies.append(copy)

    def last(c):
        if c < 2:
            return taken(6 + c)
        first, second = taken(8 + 2 * (c - 2)), taken(9 + 2 * (c - 2))
        return jnp.where(lane < 64, pltpu.roll(first, 64, 1), second)

    for i in range(3):
        solved = full_dot(f_ref[...], last(i)) + full_dot(g_ref[...], last(3 + i))
        both = full_dot(w_ref[...], solved / e_ref[...])
        l_ref[i] = both[:8]
        l_ref[3 + i] = both[8:]
    for copy in copies:
        copy.wait()


def own_row(spectra, damping, last_damping, forward, forward_slope, inverse, slab_inverse, samples, spans):
    whole = pl.BlockSpec(memory_space=pltpu.VMEM)
    return pl.pallas_call(
        functools.partial(row_kernel, spans),
        in_specs=[whole] * 7,
        out_specs=(pl.BlockSpec(memory_space=pltpu.HBM), whole),
        out_shape=(
            pltpu.HBM((samples * spans, 3, 3, 8, 128), jnp.float32),
            jax.ShapeDtypeStruct((6, 8, 128), jnp.float32),
        ),
        scratch_shapes=[
            pltpu.VMEM((3, spans, 3, 8, 128), jnp.float32),
            pltpu.SemaphoreType.DMA((3, samples)),
        ],
        compiler_params=pltpu.CompilerParams(vmem_limit_bytes=32 * 1024 * 1024),
    )(spectra, damping, last_damping, forward, forward_slope, inverse, slab_inverse)


def slab_kernel(r_ref, l_ref, t_ref, c_ref, x_ref, v_ref, g_ref):
    i = pl.program_id(0)
    rows = r_ref.shape[0]
    _, size_y, slab, size_x = v_ref.shape
    flat = r_ref.reshape(rows * 3 * slab, 128)
    column = jnp.broadcast_to(c_ref[...], (c_ref.shape[0], 128))
    out_v = v_ref.reshape(size_y * slab, size_x)
    out_g = g_ref.reshape(3, size_y * slab, size_x)
    lane = lax.broadcasted_iota(jnp.int32, (rows, 128), 1)
    half = t_ref.shape[0] // 2
    for first in range(0, slab, 2):
        values, slopes = [], []
        for z in (first, first + 1):
            value, slope, high = [
                flat[pl.ds(slab * part + z, rows, stride=3 * slab), :] for part in range(3)
            ]
            value_high = jnp.where(lane < 64, high, 0.0)
            slope_high = jnp.where(lane < 64, pltpu.roll(high, 64, 1), 0.0)
            values.append(jnp.concatenate([value, value_high], axis=1))
            slopes.append(jnp.concatenate([slope, slope_high], axis=1))
        across = (((1,), (1,)), ((), ()))
        value = lax.dot_general(
            t_ref[...],
            three_of(jnp.concatenate(values, axis=0), 1),
            across,
            preferred_element_type=jnp.float32,
        )
        slope = lax.dot_general(
            t_ref[:half],
            three_of(jnp.concatenate(slopes, axis=0), 1),
            across,
            preferred_element_type=jnp.float32,
        )
        for k, z in enumerate((first, first + 1)):
            place = pl.ds(z, size_y, stride=slab)
            lanes = slice(k * rows, k * rows + rows)
            value_z = value[:, lanes] + column * l_ref[i, pl.ds(z, 1), :]
            slope_z = slope[:, lanes] + column[:half] * l_ref[3 + i, pl.ds(z, 1), :]
            both = jnp.dot(
                three_of(value_z[:half], 1), x_ref[...], preferred_element_type=jnp.float32
            )
            out_v[place, :] = both[:size_y, :size_x]
            out_g[0, place, :] = both[:size_y, size_x:]
            both = jnp.dot(
                three_of(jnp.concatenate([value_z[half:], slope_z], axis=0), 1),
                x_ref[:, :size_x],
                preferred_element_type=jnp.float32,
            )
            out_g[1, place, :] = both[:size_y]
            out_g[2, place, :] = both[half : half + size_y]


def slab_values(rows, last, wall_table, last_column, table_x, size_y):
    count = rows.shape[0]
    slab, size_x = rows.shape[3], table_x.shape[1] // 2
    whole = pl.BlockSpec(memory_space=pltpu.VMEM)

    return pl.pallas_call(
        slab_kernel,
        grid=(3,),
        in_specs=[
            pl.BlockSpec((count, 1, 3, slab, 128), lambda i: (0, i, 0, 0, 0)),
            whole,
            whole,
            whole,
            whole,
        ],
        out_specs=(
            pl.BlockSpec((1, size_y, slab, size_x), lambda i: (i, 0, 0, 0)),
            pl.BlockSpec((3, size_y, slab, size_x), lambda i: (i, 0, 0, 0)),
        ),
        out_shape=(
            jax.ShapeDtypeStruct((3, size_y, slab, size_x), jnp.float32),
            jax.ShapeDtypeStruct((9, size_y, slab, size_x), jnp.float32),
        ),
        compiler_params=pltpu.CompilerParams(vmem_limit_bytes=60 * 1024 * 1024),
    )(rows, last, wall_table, last_column, table_x)


def summed(planes, beside):
    count = lax.axis_size("sample")
    ring = count // 2
    index = lax.axis_index("sample")
    place = index % ring
    quarters = planes.reshape((ring, planes.shape[0] // ring) + planes.shape[1:])

    def shifted(values, k):
        pairs = [(i, i - i % ring + (i + k) % ring) for i in range(count)]
        return lax.ppermute(values, "sample", pairs)

    ahead = lax.dynamic_slice_in_dim(
        jnp.concatenate([quarters, quarters]), place, ring, axis=0
    )
    total = ahead[0]
    for part in [shifted(ahead[k], k) for k in range(1, ring)]:
        total = total + part
    pairs = [(i, (i + ring) % count) for i in range(count)]
    total = total + lax.ppermute(total, "sample", pairs)
    total, beside = lax.optimization_barrier((total, beside))
    parts = [shifted(total, k) for k in range(ring - 1, 0, -1)] + [total]
    start = (ring - 1 - place) % ring
    gathered = lax.dynamic_slice_in_dim(jnp.stack(parts + parts), start, ring, axis=0)
    return gathered.reshape(planes.shape), beside


def on_device(
    fields, wiener, velocity, gradient, wall_derivative, to_modes, from_modes, mode_rates
):
    size_x, slab, size_y = fields.shape[2:]
    samples = lax.axis_size("sample")
    spans = lax.axis_size("span")
    size_z = slab * spans
    step_x = LENGTH_X / size_x
    step_z = LENGTH_Z / size_z
    coupling = TIME_STEP * POLYMER_WEIGHT
    relax = TIME_STEP / (2.0 * WEISSENBERG)

    rows_x, slope_rows_x, square_x = real_basis(size_x, LENGTH_X)
    rows_z, slope_rows_z, square_z = real_basis(size_z, LENGTH_Z)
    order = np.array([slab * (d % spans) + d // spans for d in range(samples * spans)])

    field = jnp.transpose(fields[:, 0], (2, 0, 3, 1))
    ahead = [(i, (i + 1) % spans) for i in range(spans)]
    back = [((i + 1) % spans, i) for i in range(spans)]
    below = lax.ppermute(field[-1], "span", ahead)
    above = lax.ppermute(field[0], "span", back)
    speed = jnp.transpose(velocity, (0, 3, 2, 1))
    free = spring_free(
        field,
        jnp.transpose(wiener[:, 0], (0, 3, 2, 1)),
        speed,
        jnp.transpose(gradient, (0, 3, 2, 1)),
        below,
        above,
        wall_derivative,
        step_x,
        step_z,
    )
    total_square, free = summed(jnp.sum(field * field, axis=1), free)
    slab_spring = 1.0 / (1.0 - total_square / samples / EXTENSIBILITY)
    new_fields = free - relax * slab_spring[:, None] * field
    moved = lax.all_to_all(new_fields, "sample", 0, 0, tiled=True)

    own_velocity = lax.dynamic_index_in_dim(
        speed, lax.axis_index("sample"), 2, keepdims=False
    )
    modes = padded(to_modes, LANES, size_y)
    modes_slope = coupling * jnp.dot(modes, wall_derivative, precision=FULL)
    modes_velocity = jnp.einsum("my,cyx->cmx", modes, own_velocity, precision=FULL)
    modes_table = jnp.concatenate([coupling * modes, modes_slope])
    spring = lax.dynamic_index_in_dim(
        slab_spring, lax.axis_index("sample"), 0, keepdims=False
    )
    message = own_plane(
        moved,
        spring,
        modes_velocity,
        split_three(padded(modes_table, 2 * LANES, LANES), 1),
        f32(np.concatenate([rows_x, slope_rows_x @ rows_x], axis=1)),
    )
    spectra = lax.all_to_all(message, BOTH, 0, 0, tiled=True)

    row = lax.axis_index("sample") * spans + lax.axis_index("span")
    square_row = lax.dynamic_index_in_dim(f32(square_x), row, 0, keepdims=False)
    rates = padded(mode_rates[None, :], 1, LANES)
    damping = 1.0 + TIME_STEP * VISCOSITY * (
        square_row + f32(square_z)[:, None] + rates
    )
    last_damping = 1.0 + TIME_STEP * VISCOSITY * (
        f32(square_x)[None, :] + f32(square_z)[:, None] + mode_rates[size_y - 1]
    )
    inverse = np.stack([rows_z.T, rows_z.T @ slope_rows_z])
    slab_inverse = lax.dynamic_index_in_dim(
        f32(inverse.reshape(2, spans, slab, size_z)), lax.axis_index("span"), 1, keepdims=False
    ).reshape(2 * slab, size_z)
    back, last = own_row(
        spectra,
        damping,
        last_damping,
        f32(rows_z[:, order]),
        f32((slope_rows_z @ rows_z)[:, order]),
        f32(inverse.reshape(2 * size_z, size_z)),
        slab_inverse,
        samples,
        spans,
    )
    rows = lax.all_to_all(back, BOTH, 0, 0, tiled=True)

    modes_wall = jnp.dot(wall_derivative, from_modes, precision=FULL)
    wall_table = jnp.concatenate(
        [padded(from_modes, 208, LANES), padded(modes_wall, 208, LANES)]
    )
    new_velocity, new_gradient = slab_values(
        rows,
        last,
        split_three(wall_table.at[:, size_y - 1].set(0.0), 1),
        wall_table[:, size_y - 1 : size_y],
        stacked_three(np.concatenate([rows_x, (rows_x.T @ slope_rows_x).T], axis=1)),
        size_y,
    )
    return (
        jnp.transpose(new_fields, (1, 3, 0, 2))[:, None],
        jnp.transpose(new_velocity, (0, 3, 2, 1)),
        jnp.transpose(new_gradient, (0, 3, 2, 1)),
    )


def solution(mesh):
    in_specs = (
        P(None, "sample", None, "span", None),
        P(None, "sample", None, "span", None),
        P(None, None, "span", None),
        P(None, None, "span", None),
        P(),
        P(),
        P(),
        P(),
    )
    out_specs = (
        P(None, "sample", None, "span", None),
        P(None, None, "span", None),
        P(None, None, "span", None),
    )
    return jax.shard_map(
        on_device, mesh=mesh, in_specs=in_specs, out_specs=out_specs, check_vma=False
    )
```

```python
import functools
import math

import jax
import jax.numpy as jnp
import numpy as np
from jax import lax
from jax.experimental import pallas as pl
from jax.experimental.pallas import tpu as pltpu
from jax.sharding import PartitionSpec as P

TIME_STEP = 0.01
WEISSENBERG = 0.05
EXTENSIBILITY = 10.0
POLYMER_WEIGHT = 5.0
VISCOSITY = 0.5
DIFFUSIVITY = 0.003
LENGTH_X = math.pi
LENGTH_Z = 2.0 * math.pi / 3.0
FULL = lax.Precision.HIGHEST
HIGH = lax.Precision.HIGH
BOTH = ("sample", "span")
LANES = 256
PAIRS = ((0, 0), (0, 1), (0, 2), (1, 1), (1, 2), (2, 2))
COLUMN = ((0, 1, 2), (1, 3, 4), (2, 4, 5))


def real_basis(count, extent):
    half = count // 2
    place = np.arange(count)
    rows = np.zeros((count, count))
    kappa = np.zeros(count)
    slope = np.zeros((count, count))
    unit = 2.0 * math.pi / extent
    rows[0] = math.sqrt(1.0 / count)
    for k in range(1, half):
        angle = 2.0 * math.pi * ((k * place) % count) / count
        rows[k] = math.sqrt(2.0 / count) * np.cos(angle)
        rows[half + k] = math.sqrt(2.0 / count) * np.sin(angle)
        kappa[k] = kappa[half + k] = unit * k
        slope[k, half + k] = unit * k
        slope[half + k, k] = -unit * k
    rows[half] = math.sqrt(1.0 / count) * (1.0 - 2.0 * (place % 2))
    kappa[half] = unit * half
    return rows, slope, kappa * kappa


def f32(values):
    return jnp.asarray(np.asarray(values, np.float32))


def slope_kernel(f_ref, d_ref, e_ref, o_ref):
    size_x = f_ref.shape[3]
    for i in range(3):
        pair = jnp.concatenate([f_ref[0, i], f_ref[1, i]], axis=1)
        high = pair.astype(jnp.bfloat16)
        low = (pair - high.astype(jnp.float32)).astype(jnp.bfloat16)
        slope = jnp.dot(d_ref[...], high, preferred_element_type=jnp.float32)
        slope += jnp.dot(d_ref[...], low, preferred_element_type=jnp.float32)
        slope += jnp.dot(e_ref[...], high, preferred_element_type=jnp.float32)
        o_ref[0, i] = slope[:, :size_x]
        o_ref[1, i] = slope[:, size_x:]


def wall_slope(planes, wall_derivative):
    slab, _, size_y, size_x = planes.shape
    high = lax.reduce_precision(wall_derivative, 8, 7)
    low = (wall_derivative - high).astype(jnp.bfloat16)
    whole = pl.BlockSpec(memory_space=pltpu.VMEM)
    pair = pl.BlockSpec((2, 3, size_y, size_x), lambda j: (j, 0, 0, 0))
    return pl.pallas_call(
        slope_kernel,
        grid=(slab // 2,),
        in_specs=[pair, whole, whole],
        out_specs=pair,
        out_shape=pltpu.HBM(planes.shape, jnp.float32),
        compiler_params=pltpu.CompilerParams(vmem_limit_bytes=24 * 1024 * 1024),
        cost_estimate=pl.CostEstimate(flops=10**9, bytes_accessed=6 * 10**6, transcendentals=0),
    )(planes, high.astype(jnp.bfloat16), low)


def free_kernel(scales, p_ref, s_ref, w_ref, v_ref, g_ref, lo_ref, hi_ref, o_ref):
    scale_x, scale_z, scale_c, scale_w = scales
    slab, _, block, size_x = p_ref.shape
    noise, speed, tensor = [
        r.reshape(r.shape[0], block * slab, size_x) for r in (w_ref, v_ref, g_ref)
    ]
    for z in range(slab):
        plane = pl.ds(z, block, stride=slab)
        speed_x, speed_y, speed_z = [speed[c, plane, :] for c in range(3)]
        parts = [p_ref[z, c] for c in range(3)]
        for i in range(3):
            own = parts[i]
            upper = hi_ref[i] if z == slab - 1 else p_ref[z + 1, i]
            lower = lo_ref[i] if z == 0 else p_ref[z - 1, i]
            slope_x = pltpu.roll(own, size_x - 1, 1) - pltpu.roll(own, 1, 1)
            advect = (
                speed_x * (scale_x * slope_x)
                + speed_y * s_ref[z, i]
                + speed_z * (scale_z * (upper - lower))
            )
            stretch = (
                tensor[3 * i, plane, :] * parts[0]
                + tensor[3 * i + 1, plane, :] * parts[1]
                + tensor[3 * i + 2, plane, :] * parts[2]
            )
            result = own + TIME_STEP * (stretch - advect)
            result = result + scale_c * (upper - 2.0 * own + lower)
            o_ref[z, i] = result + scale_w * noise[i, plane, :]


def spring_free(planes, slope, wiener, velocity, gradient, below, above, step_x, step_z):
    slab, _, size_y, size_x = planes.shape
    block = 40
    scales = (
        1.0 / (2.0 * step_x),
        1.0 / (2.0 * step_z),
        DIFFUSIVITY * TIME_STEP / (step_z * step_z),
        math.sqrt(TIME_STEP / WEISSENBERG),
    )

    def rows(count):
        return pl.BlockSpec((count, block, slab, size_x), lambda j: (0, j, 0, 0))

    across = pl.BlockSpec((slab, 3, block, size_x), lambda j: (0, 0, j, 0))
    edge = pl.BlockSpec((3, block, size_x), lambda j: (0, j, 0))
    return pl.pallas_call(
        functools.partial(free_kernel, scales),
        grid=(-(-size_y // block),),
        in_specs=[across, across, rows(3), rows(3), rows(9), edge, edge],
        out_specs=across,
        out_shape=pltpu.HBM(planes.shape, jnp.float32),
        compiler_params=pltpu.CompilerParams(vmem_limit_bytes=60 * 1024 * 1024),
        cost_estimate=pl.CostEstimate(flops=10**8, bytes_accessed=19 * 10**6, transcendentals=0),
    )(planes, slope, wiener, velocity, gradient, below, above)


def padded(values, rows, columns):
    return jnp.pad(
        values, ((0, rows - values.shape[0]), (0, columns - values.shape[1]))
    )


def stacked_three(table):
    table = np.asarray(table, np.float32)
    high = table.astype(jnp.bfloat16)
    low = (table - high.astype(np.float32)).astype(jnp.bfloat16)
    return jnp.asarray(np.concatenate([high, high, low], axis=0))


def split_three(table, axis):
    high = lax.reduce_precision(table, 8, 7)
    low = (table - high).astype(jnp.bfloat16)
    high = high.astype(jnp.bfloat16)
    return jnp.concatenate([high, high, low], axis=axis)


def three_of(values, axis):
    high = values.astype(jnp.bfloat16)
    low = (values - high.astype(jnp.float32)).astype(jnp.bfloat16)
    return jnp.concatenate([high, low, high], axis=axis)


def full_dot(a, b, side=0):
    return lax.dot_general(
        a,
        b,
        (((1,), (side,)), ((), ())),
        precision=FULL,
        preferred_element_type=jnp.float32,
    )


def plane_kernel(n_ref, s_ref, v_ref, m_ref, x_ref, o_ref, t_ref):
    k = pl.program_id(0)
    count = pl.num_programs(0)
    size_y, size_x = s_ref.shape

    @pl.when(k == 0)
    def _():
        t_ref[...] = jnp.zeros_like(t_ref)

    for start in range(0, size_y, 64):
        part = pl.ds(start, min(64, size_y - start))
        moved = [n_ref[0, c, part, :] for c in range(3)]
        for p, (i, j) in enumerate(PAIRS):
            t_ref[p, part, :] += moved[i] * moved[j]

    @pl.when(k == count - 1)
    def _():
        for start in range(0, size_y, 64):
            part = pl.ds(start, min(64, size_y - start))
            spring = s_ref[part, :]
            for p, (i, j) in enumerate(PAIRS):
                value = spring * (t_ref[p, part, :] / count)
                t_ref[p, part, :] = value - 1.0 if i == j else value
        scaled, slope = m_ref[:LANES, :], m_ref[LANES:, :]
        last_mode = size_y - 1
        rest = [None] * 6
        for i in range(3):
            column = [t_ref[p] for p in COLUMN[i]]
            direct = v_ref[i] + jnp.dot(
                slope, three_of(column[1], 0), preferred_element_type=jnp.float32
            )
            along = jnp.dot(
                scaled,
                three_of(jnp.concatenate([column[0], column[2]], axis=1), 0),
                preferred_element_type=jnp.float32,
            )
            force = full_dot(
                x_ref[...], jnp.concatenate([direct, along[:, :size_x]], axis=1), 1
            )
            force_z = full_dot(x_ref[:, :size_x], along[:, size_x:], 1)
            top = slice(last_mode, last_mode + 8)
            own = jnp.concatenate([direct[top], along[top, :size_x]], axis=1)
            rest[i] = full_dot(own, x_ref[...], 1)[:1]
            rest[3 + i] = full_dot(along[top, size_x:], x_ref[:, :size_x], 1)[:1]
            for half in range(2):
                lanes = slice(half * 128, half * 128 + 128)
                o_ref[pl.ds(8 * half + i, 128, stride=16), :] = force[:, lanes]
                o_ref[pl.ds(8 * half + 3 + i, 128, stride=16), :] = force_z[:, lanes]
        lane = lax.broadcasted_iota(jnp.int32, (128, 128), 1)
        for c in range(2):
            o_ref[pl.ds(6 + c, 128, stride=16), :] = jnp.broadcast_to(rest[c], (128, 128))
        for c in range(4):
            for part in range(2):
                row = jnp.broadcast_to(rest[2 + c], (128, 128))
                row = row if part else pltpu.roll(row, 64, 1)
                place = pl.ds(8 + 2 * c + part, 128, stride=16)
                kept = o_ref[place, :] if 2 * c + part < 6 else jnp.zeros_like(row)
                o_ref[place, :] = jnp.where(lane < 64, kept, row)


def own_plane(moved, spring, modes_velocity, modes, rows):
    count, _, size_y, size_x = moved.shape
    whole = pl.BlockSpec(memory_space=pltpu.VMEM)
    message = pl.pallas_call(
        plane_kernel,
        grid=(count,),
        in_specs=[
            pl.BlockSpec((1, 3, size_y, size_x), lambda k: (k, 0, 0, 0)),
            whole,
            whole,
            whole,
            whole,
        ],
        out_specs=pl.BlockSpec((size_x * 16, 128), lambda k: (0, 0)),
        out_shape=jax.ShapeDtypeStruct((size_x * 16, 128), jnp.float32),
        scratch_shapes=[pltpu.VMEM((6, LANES, size_x), jnp.float32)],
        compiler_params=pltpu.CompilerParams(vmem_limit_bytes=24 * 1024 * 1024),
    )(moved, spring, modes_velocity, modes, rows)
    return message.reshape(size_x, 2, 8, 128)


def row_kernel(spans, in_ref, d_ref, e_ref, f_ref, g_ref, b_ref, w_ref, o_ref, l_ref, t_ref, sem):
    flat = in_ref.reshape(in_ref.shape[0] * 16, 128)
    lane = lax.broadcasted_iota(jnp.int32, (128, 128), 1)

    def taken(c):
        return flat[pl.ds(c, 128, stride=16), :]

    def loaded(c):
        return jnp.concatenate([taken(c), taken(8 + c)], axis=1)

    samples = o_ref.shape[0] // spans
    copies = []
    for i in range(3):
        solved = full_dot(f_ref[...], loaded(i)) + full_dot(g_ref[...], loaded(3 + i))
        both = full_dot(b_ref[...], solved / d_ref[...])
        value, slope = both[:128], both[128:]
        t_ref[i, :, 0] = value[:, :128].reshape(spans, 8, 128)
        t_ref[i, :, 1] = slope[:, :128].reshape(spans, 8, 128)
        mixed = jnp.where(lane < 64, value[:, 128:], pltpu.roll(slope[:, 128:], 64, 1))
        t_ref[i, :, 2] = mixed.reshape(spans, 8, 128)
        for k in range(samples):
            copy = pltpu.make_async_copy(
                t_ref.at[i], o_ref.at[pl.ds(k * spans, spans), i], sem.at[i, k]
            )
            copy.start()
            copies.append(copy)

    def last(c):
        if c < 2:
            return taken(6 + c)
        first, second = taken(8 + 2 * (c - 2)), taken(9 + 2 * (c - 2))
        return jnp.where(lane < 64, pltpu.roll(first, 64, 1), second)

    for i in range(3):
        solved = full_dot(f_ref[...], last(i)) + full_dot(g_ref[...], last(3 + i))
        both = full_dot(w_ref[...], solved / e_ref[...])
        l_ref[i] = both[:8]
        l_ref[3 + i] = both[8:]
    for copy in copies:
        copy.wait()


def own_row(spectra, damping, last_damping, forward, forward_slope, inverse, slab_inverse, samples, spans):
    whole = pl.BlockSpec(memory_space=pltpu.VMEM)
    return pl.pallas_call(
        functools.partial(row_kernel, spans),
        in_specs=[whole] * 7,
        out_specs=(pl.BlockSpec(memory_space=pltpu.HBM), whole),
        out_shape=(
            pltpu.HBM((samples * spans, 3, 3, 8, 128), jnp.float32),
            jax.ShapeDtypeStruct((6, 8, 128), jnp.float32),
        ),
        scratch_shapes=[
            pltpu.VMEM((3, spans, 3, 8, 128), jnp.float32),
            pltpu.SemaphoreType.DMA((3, samples)),
        ],
        compiler_params=pltpu.CompilerParams(vmem_limit_bytes=32 * 1024 * 1024),
    )(spectra, damping, last_damping, forward, forward_slope, inverse, slab_inverse)


def slab_kernel(r_ref, l_ref, t_ref, c_ref, x_ref, v_ref, g_ref):
    i = pl.program_id(0)
    rows = r_ref.shape[0]
    _, size_y, slab, size_x = v_ref.shape
    flat = r_ref.reshape(rows * 3 * slab, 128)
    column = jnp.broadcast_to(c_ref[...], (c_ref.shape[0], 128))
    out_v = v_ref.reshape(size_y * slab, size_x)
    out_g = g_ref.reshape(3, size_y * slab, size_x)
    lane = lax.broadcasted_iota(jnp.int32, (rows, 128), 1)
    half = t_ref.shape[0] // 2
    for first in range(0, slab, 2):
        values, slopes = [], []
        for z in (first, first + 1):
            value, slope, high = [
                flat[pl.ds(slab * part + z, rows, stride=3 * slab), :] for part in range(3)
            ]
            value_high = jnp.where(lane < 64, high, 0.0)
            slope_high = jnp.where(lane < 64, pltpu.roll(high, 64, 1), 0.0)
            values.append(jnp.concatenate([value, value_high], axis=1))
            slopes.append(jnp.concatenate([slope, slope_high], axis=1))
        across = (((1,), (1,)), ((), ()))
        value = lax.dot_general(
            t_ref[...],
            three_of(jnp.concatenate(values, axis=0), 1),
            across,
            preferred_element_type=jnp.float32,
        )
        slope = lax.dot_general(
            t_ref[:half],
            three_of(jnp.concatenate(slopes, axis=0), 1),
            across,
            preferred_element_type=jnp.float32,
        )
        for k, z in enumerate((first, first + 1)):
            place = pl.ds(z, size_y, stride=slab)
            lanes = slice(k * rows, k * rows + rows)
            value_z = value[:, lanes] + column * l_ref[i, pl.ds(z, 1), :]
            slope_z = slope[:, lanes] + column[:half] * l_ref[3 + i, pl.ds(z, 1), :]
            both = jnp.dot(
                three_of(value_z[:half], 1), x_ref[...], preferred_element_type=jnp.float32
            )
            out_v[place, :] = both[:size_y, :size_x]
            out_g[0, place, :] = both[:size_y, size_x:]
            both = jnp.dot(
                three_of(jnp.concatenate([value_z[half:], slope_z], axis=0), 1),
                x_ref[:, :size_x],
                preferred_element_type=jnp.float32,
            )
            out_g[1, place, :] = both[:size_y]
            out_g[2, place, :] = both[half : half + size_y]


def slab_values(rows, last, wall_table, last_column, table_x, size_y):
    count = rows.shape[0]
    slab, size_x = rows.shape[3], table_x.shape[1] // 2
    whole = pl.BlockSpec(memory_space=pltpu.VMEM)

    return pl.pallas_call(
        slab_kernel,
        grid=(3,),
        in_specs=[
            pl.BlockSpec((count, 1, 3, slab, 128), lambda i: (0, i, 0, 0, 0)),
            whole,
            whole,
            whole,
            whole,
        ],
        out_specs=(
            pl.BlockSpec((1, size_y, slab, size_x), lambda i: (i, 0, 0, 0)),
            pl.BlockSpec((3, size_y, slab, size_x), lambda i: (i, 0, 0, 0)),
        ),
        out_shape=(
            jax.ShapeDtypeStruct((3, size_y, slab, size_x), jnp.float32),
            jax.ShapeDtypeStruct((9, size_y, slab, size_x), jnp.float32),
        ),
        compiler_params=pltpu.CompilerParams(vmem_limit_bytes=60 * 1024 * 1024),
    )(rows, last, wall_table, last_column, table_x)


def summed(planes, early, rest):
    count = lax.axis_size("sample")
    ring = count // 2
    index = lax.axis_index("sample")
    place = index % ring
    quarters = planes.reshape((ring, planes.shape[0] // ring) + planes.shape[1:])

    def shifted(values, k):
        pairs = [(i, i - i % ring + (i + k) % ring) for i in range(count)]
        return lax.ppermute(values, "sample", pairs)

    ahead = lax.dynamic_slice_in_dim(
        jnp.concatenate([quarters, quarters]), place, ring, axis=0
    )
    total = ahead[0]
    for part in [shifted(ahead[k], k) for k in range(1, ring)]:
        total = total + part
    total, early = lax.optimization_barrier((total, early))
    pairs = [(i, (i + ring) % count) for i in range(count)]
    total = total + lax.ppermute(total, "sample", pairs)
    total, beside = lax.optimization_barrier((total, rest(early)))
    return place, [total] + [shifted(total, k) for k in range(1, ring)], beside


def finish_kernel(relax, samples, at_ref, *refs):
    *quarters, a_ref, f_ref, o_ref, s_ref = refs
    for k, quarter in enumerate(quarters):

        @pl.when(pl.program_id(0) == k)
        def _(quarter=quarter):
            for j in range(quarter.shape[0]):
                spring = 1.0 / (1.0 - quarter[j] / samples / EXTENSIBILITY)
                s_ref[j] = spring
                scale = relax * spring
                for c in range(3):
                    o_ref[j, c] = a_ref[j, c] - scale * f_ref[j, c]


def finished(place, quarters, free, planes, relax, samples):
    slab, _, size_y, size_x = planes.shape
    ring = len(quarters)
    part = slab // ring
    whole = pl.BlockSpec(memory_space=pltpu.VMEM)

    def quarter(k, at):
        return lax.rem(at[0] + ring - k, ring)

    each = pl.BlockSpec((part, 3, size_y, size_x), lambda k, at: (quarter(k, at), 0, 0, 0))
    return pl.pallas_call(
        functools.partial(finish_kernel, relax, samples),
        grid_spec=pltpu.PrefetchScalarGridSpec(
            num_scalar_prefetch=1,
            grid=(ring,),
            in_specs=[whole] * ring + [each, each],
            out_specs=(
                each,
                pl.BlockSpec((part, size_y, size_x), lambda k, at: (quarter(k, at), 0, 0)),
            ),
        ),
        out_shape=(
            pltpu.HBM(planes.shape, jnp.float32),
            jax.ShapeDtypeStruct((slab, size_y, size_x), jnp.float32),
        ),
        compiler_params=pltpu.CompilerParams(vmem_limit_bytes=60 * 1024 * 1024),
    )(jnp.reshape(place, (1,)).astype(jnp.int32), *quarters, free, planes)


def on_device(
    fields, wiener, velocity, gradient, wall_derivative, to_modes, from_modes, mode_rates
):
    size_x, slab, size_y = fields.shape[2:]
    samples = lax.axis_size("sample")
    spans = lax.axis_size("span")
    size_z = slab * spans
    step_x = LENGTH_X / size_x
    step_z = LENGTH_Z / size_z
    coupling = TIME_STEP * POLYMER_WEIGHT
    relax = TIME_STEP / (2.0 * WEISSENBERG)

    rows_x, slope_rows_x, square_x = real_basis(size_x, LENGTH_X)
    rows_z, slope_rows_z, square_z = real_basis(size_z, LENGTH_Z)
    order = np.array([slab * (d % spans) + d // spans for d in range(samples * spans)])

    field = jnp.transpose(fields[:, 0], (2, 0, 3, 1))
    ahead = [(i, (i + 1) % spans) for i in range(spans)]
    back = [((i + 1) % spans, i) for i in range(spans)]
    below = lax.ppermute(field[-1], "span", ahead)
    above = lax.ppermute(field[0], "span", back)
    speed = jnp.transpose(velocity, (0, 3, 2, 1))

    def rest(slope):
        return spring_free(
            field,
            slope,
            jnp.transpose(wiener[:, 0], (0, 3, 2, 1)),
            speed,
            jnp.transpose(gradient, (0, 3, 2, 1)),
            below,
            above,
            step_x,
            step_z,
        )

    slope = wall_slope(field, wall_derivative)
    place, quarters, free = summed(jnp.sum(field * field, axis=1), slope, rest)
    new_fields, slab_spring = finished(place, quarters, free, field, relax, samples)
    moved = lax.all_to_all(new_fields, "sample", 0, 0, tiled=True)

    own_velocity = lax.dynamic_index_in_dim(
        speed, lax.axis_index("sample"), 2, keepdims=False
    )
    modes = padded(to_modes, LANES, size_y)
    modes_slope = coupling * jnp.dot(modes, wall_derivative, precision=FULL)
    modes_velocity = jnp.einsum("my,cyx->cmx", modes, own_velocity, precision=FULL)
    modes_table = jnp.concatenate([coupling * modes, modes_slope])
    spring = lax.dynamic_index_in_dim(
        slab_spring, lax.axis_index("sample"), 0, keepdims=False
    )
    message = own_plane(
        moved,
        spring,
        modes_velocity,
        split_three(padded(modes_table, 2 * LANES, LANES), 1),
        f32(np.concatenate([rows_x, slope_rows_x @ rows_x], axis=1)),
    )
    spectra = lax.all_to_all(message, BOTH, 0, 0, tiled=True)

    row = lax.axis_index("sample") * spans + lax.axis_index("span")
    square_row = lax.dynamic_index_in_dim(f32(square_x), row, 0, keepdims=False)
    rates = padded(mode_rates[None, :], 1, LANES)
    damping = 1.0 + TIME_STEP * VISCOSITY * (
        square_row + f32(square_z)[:, None] + rates
    )
    last_damping = 1.0 + TIME_STEP * VISCOSITY * (
        f32(square_x)[None, :] + f32(square_z)[:, None] + mode_rates[size_y - 1]
    )
    inverse = np.stack([rows_z.T, rows_z.T @ slope_rows_z])
    slab_inverse = lax.dynamic_index_in_dim(
        f32(inverse.reshape(2, spans, slab, size_z)), lax.axis_index("span"), 1, keepdims=False
    ).reshape(2 * slab, size_z)
    back, last = own_row(
        spectra,
        damping,
        last_damping,
        f32(rows_z[:, order]),
        f32((slope_rows_z @ rows_z)[:, order]),
        f32(inverse.reshape(2 * size_z, size_z)),
        slab_inverse,
        samples,
        spans,
    )
    rows = lax.all_to_all(back, BOTH, 0, 0, tiled=True)

    modes_wall = jnp.dot(wall_derivative, from_modes, precision=FULL)
    wall_table = jnp.concatenate(
        [padded(from_modes, 208, LANES), padded(modes_wall, 208, LANES)]
    )
    new_velocity, new_gradient = slab_values(
        rows,
        last,
        split_three(wall_table.at[:, size_y - 1].set(0.0), 1),
        wall_table[:, size_y - 1 : size_y],
        stacked_three(np.concatenate([rows_x, (rows_x.T @ slope_rows_x).T], axis=1)),
        size_y,
    )
    return (
        jnp.transpose(new_fields, (1, 3, 0, 2))[:, None],
        jnp.transpose(new_velocity, (0, 3, 2, 1)),
        jnp.transpose(new_gradient, (0, 3, 2, 1)),
    )


def solution(mesh):
    in_specs = (
        P(None, "sample", None, "span", None),
        P(None, "sample", None, "span", None),
        P(None, None, "span", None),
        P(None, None, "span", None),
        P(),
        P(),
        P(),
        P(),
    )
    out_specs = (
        P(None, "sample", None, "span", None),
        P(None, None, "span", None),
        P(None, None, "span", None),
    )
    return jax.shard_map(
        on_device, mesh=mesh, in_specs=in_specs, out_specs=out_specs, check_vma=False
    )
```

```python
import functools
import math

import jax
import jax.numpy as jnp
import numpy as np
from jax import lax
from jax.experimental import pallas as pl
from jax.experimental.pallas import tpu as pltpu
from jax.sharding import PartitionSpec as P

TIME_STEP = 0.01
WEISSENBERG = 0.05
EXTENSIBILITY = 10.0
POLYMER_WEIGHT = 5.0
VISCOSITY = 0.5
DIFFUSIVITY = 0.003
LENGTH_X = math.pi
LENGTH_Z = 2.0 * math.pi / 3.0
FULL = lax.Precision.HIGHEST
HIGH = lax.Precision.HIGH
BOTH = ("sample", "span")
LANES = 256
PAIRS = ((0, 0), (0, 1), (0, 2), (1, 1), (1, 2), (2, 2))
COLUMN = ((0, 1, 2), (1, 3, 4), (2, 4, 5))


def real_basis(count, extent):
    half = count // 2
    place = np.arange(count)
    rows = np.zeros((count, count))
    kappa = np.zeros(count)
    slope = np.zeros((count, count))
    unit = 2.0 * math.pi / extent
    rows[0] = math.sqrt(1.0 / count)
    for k in range(1, half):
        angle = 2.0 * math.pi * ((k * place) % count) / count
        rows[k] = math.sqrt(2.0 / count) * np.cos(angle)
        rows[half + k] = math.sqrt(2.0 / count) * np.sin(angle)
        kappa[k] = kappa[half + k] = unit * k
        slope[k, half + k] = unit * k
        slope[half + k, k] = -unit * k
    rows[half] = math.sqrt(1.0 / count) * (1.0 - 2.0 * (place % 2))
    kappa[half] = unit * half
    return rows, slope, kappa * kappa


def f32(values):
    return jnp.asarray(np.asarray(values, np.float32))


def free_kernel(
    scales, f_ref, p_ref, w_ref, v_ref, g_ref, lo_ref, hi_ref, d_ref, e_ref, o_ref, s_ref
):
    scale_x, scale_z, scale_c, scale_w = scales
    slab, _, size_y, size_x = f_ref.shape
    block = p_ref.shape[2]
    here = pl.ds(pl.multiple_of(pl.program_id(0) * block, 8), block)

    @pl.when(pl.program_id(0) == 0)
    def _():
        for i in range(3):
            for z in range(0, slab, 2):
                pair = jnp.concatenate([f_ref[z, i], f_ref[z + 1, i]], axis=1)
                high = pair.astype(jnp.bfloat16)
                low = (pair - high.astype(jnp.float32)).astype(jnp.bfloat16)
                slope = jnp.dot(d_ref[...], high, preferred_element_type=jnp.float32)
                slope += jnp.dot(d_ref[...], low, preferred_element_type=jnp.float32)
                slope += jnp.dot(e_ref[...], high, preferred_element_type=jnp.float32)
                s_ref[z, i, :size_y, :] = slope[:, :size_x]
                s_ref[z + 1, i, :size_y, :] = slope[:, size_x:]

    noise, speed, tensor = [
        r.reshape(r.shape[0], block * slab, size_x) for r in (w_ref, v_ref, g_ref)
    ]
    for z in range(slab):
        plane = pl.ds(z, block, stride=slab)
        speed_x, speed_y, speed_z = [speed[c, plane, :] for c in range(3)]
        parts = [p_ref[z, c] for c in range(3)]
        for i in range(3):
            own = parts[i]
            upper = hi_ref[i] if z == slab - 1 else p_ref[z + 1, i]
            lower = lo_ref[i] if z == 0 else p_ref[z - 1, i]
            slope_x = pltpu.roll(own, size_x - 1, 1) - pltpu.roll(own, 1, 1)
            advect = (
                speed_x * (scale_x * slope_x)
                + speed_y * s_ref[z, i, here, :]
                + speed_z * (scale_z * (upper - lower))
            )
            stretch = (
                tensor[3 * i, plane, :] * parts[0]
                + tensor[3 * i + 1, plane, :] * parts[1]
                + tensor[3 * i + 2, plane, :] * parts[2]
            )
            result = own + TIME_STEP * (stretch - advect)
            result = result + scale_c * (upper - 2.0 * own + lower)
            o_ref[z, i] = result + scale_w * noise[i, plane, :]


def spring_free(planes, wiener, velocity, gradient, below, above, wall_derivative, step_x, step_z):
    slab, _, size_y, size_x = planes.shape
    block = 40
    steps = -(-size_y // block)
    whole = pl.BlockSpec(memory_space=pltpu.VMEM)
    high = lax.reduce_precision(wall_derivative, 8, 7)
    low = (wall_derivative - high).astype(jnp.bfloat16)
    high = high.astype(jnp.bfloat16)
    scales = (
        1.0 / (2.0 * step_x),
        1.0 / (2.0 * step_z),
        DIFFUSIVITY * TIME_STEP / (step_z * step_z),
        math.sqrt(TIME_STEP / WEISSENBERG),
    )

    def rows(count):
        return pl.BlockSpec((count, block, slab, size_x), lambda j: (0, j, 0, 0))

    across = pl.BlockSpec((slab, 3, block, size_x), lambda j: (0, 0, j, 0))
    edge = pl.BlockSpec((3, block, size_x), lambda j: (0, j, 0))
    return pl.pallas_call(
        functools.partial(free_kernel, scales),
        grid=(steps,),
        in_specs=[whole, across, rows(3), rows(3), rows(9), edge, edge, whole, whole],
        out_specs=across,
        out_shape=pltpu.HBM(planes.shape, jnp.float32),
        scratch_shapes=[pltpu.VMEM((slab, 3, steps * block, size_x), jnp.float32)],
        compiler_params=pltpu.CompilerParams(vmem_limit_bytes=60 * 1024 * 1024),
        cost_estimate=pl.CostEstimate(flops=3 * 10**9, bytes_accessed=18 * 10**6, transcendentals=0),
    )(planes, planes, wiener, velocity, gradient, below, above, high, low)


def padded(values, rows, columns):
    return jnp.pad(
        values, ((0, rows - values.shape[0]), (0, columns - values.shape[1]))
    )


def stacked_three(table):
    table = np.asarray(table, np.float32)
    high = table.astype(jnp.bfloat16)
    low = (table - high.astype(np.float32)).astype(jnp.bfloat16)
    return jnp.asarray(np.concatenate([high, high, low], axis=0))


def paired_three(table):
    table = np.asarray(table, np.float32)
    high = table.astype(jnp.bfloat16)
    low = (table - high.astype(np.float32)).astype(jnp.bfloat16)
    column = np.concatenate([high, high, low], axis=0)
    empty = np.zeros_like(column)
    return jnp.asarray(
        np.concatenate(
            [np.concatenate([column, empty], axis=1), np.concatenate([empty, column], axis=1)]
        )
    )


def split_three(table, axis):
    high = lax.reduce_precision(table, 8, 7)
    low = (table - high).astype(jnp.bfloat16)
    high = high.astype(jnp.bfloat16)
    return jnp.concatenate([high, high, low], axis=axis)


def three_of(values, axis):
    high = values.astype(jnp.bfloat16)
    low = (values - high.astype(jnp.float32)).astype(jnp.bfloat16)
    return jnp.concatenate([high, low, high], axis=axis)


def full_dot(a, b, side=0):
    return lax.dot_general(
        a,
        b,
        (((1,), (side,)), ((), ())),
        precision=FULL,
        preferred_element_type=jnp.float32,
    )


def plane_kernel(n_ref, s_ref, v_ref, m_ref, x_ref, o_ref, t_ref):
    k = pl.program_id(0)
    steps = pl.num_programs(0)
    count = steps * n_ref.shape[0]
    size_y, size_x = s_ref.shape

    @pl.when(k == 0)
    def _():
        t_ref[...] = jnp.zeros_like(t_ref)

    for start in range(0, size_y, 32):
        part = pl.ds(start, min(32, size_y - start))
        moved = [[n_ref[f, c, part, :] for c in range(3)] for f in range(n_ref.shape[0])]
        for p, (i, j) in enumerate(PAIRS):
            value = moved[0][i] * moved[0][j]
            for own in moved[1:]:
                value += own[i] * own[j]
            t_ref[p, part, :] += value

    @pl.when(k == steps - 1)
    def _():
        for start in range(0, size_y, 64):
            part = pl.ds(start, min(64, size_y - start))
            spring = s_ref[part, :]
            for p, (i, j) in enumerate(PAIRS):
                value = spring * (t_ref[p, part, :] / count)
                t_ref[p, part, :] = value - 1.0 if i == j else value
        scaled, slope = m_ref[:LANES, :], m_ref[LANES:, :]
        last_mode = size_y - 1
        rest = [None] * 6
        for i in range(3):
            column = [t_ref[p] for p in COLUMN[i]]
            direct = v_ref[i] + jnp.dot(
                slope, three_of(column[1], 0), preferred_element_type=jnp.float32
            )
            along = jnp.dot(
                scaled,
                three_of(jnp.concatenate([column[0], column[2]], axis=1), 0),
                preferred_element_type=jnp.float32,
            )
            force = full_dot(
                x_ref[...], jnp.concatenate([direct, along[:, :size_x]], axis=1), 1
            )
            force_z = full_dot(x_ref[:, :size_x], along[:, size_x:], 1)
            top = slice(last_mode, last_mode + 8)
            own = jnp.concatenate([direct[top], along[top, :size_x]], axis=1)
            rest[i] = full_dot(own, x_ref[...], 1)[:1]
            rest[3 + i] = full_dot(along[top, size_x:], x_ref[:, :size_x], 1)[:1]
            for half in range(2):
                lanes = slice(half * 128, half * 128 + 128)
                o_ref[pl.ds(8 * half + i, 128, stride=16), :] = force[:, lanes]
                o_ref[pl.ds(8 * half + 3 + i, 128, stride=16), :] = force_z[:, lanes]
        lane = lax.broadcasted_iota(jnp.int32, (128, 128), 1)
        for c in range(2):
            o_ref[pl.ds(6 + c, 128, stride=16), :] = jnp.broadcast_to(rest[c], (128, 128))
        for c in range(4):
            for part in range(2):
                row = jnp.broadcast_to(rest[2 + c], (128, 128))
                row = row if part else pltpu.roll(row, 64, 1)
                place = pl.ds(8 + 2 * c + part, 128, stride=16)
                kept = o_ref[place, :] if 2 * c + part < 6 else jnp.zeros_like(row)
                o_ref[place, :] = jnp.where(lane < 64, kept, row)


def own_plane(moved, spring, modes_velocity, modes, rows):
    count, _, size_y, size_x = moved.shape
    whole = pl.BlockSpec(memory_space=pltpu.VMEM)
    message = pl.pallas_call(
        plane_kernel,
        grid=(2,),
        in_specs=[
            pl.BlockSpec((count // 2, 3, size_y, size_x), lambda k: (k, 0, 0, 0)),
            whole,
            whole,
            whole,
            whole,
        ],
        out_specs=pl.BlockSpec((size_x * 16, 128), lambda k: (0, 0)),
        out_shape=jax.ShapeDtypeStruct((size_x * 16, 128), jnp.float32),
        scratch_shapes=[pltpu.VMEM((6, LANES, size_x), jnp.float32)],
        compiler_params=pltpu.CompilerParams(vmem_limit_bytes=24 * 1024 * 1024),
    )(moved, spring, modes_velocity, modes, rows)
    return message.reshape(size_x, 2, 8, 128)


def row_kernel(spans, in_ref, d_ref, e_ref, f_ref, g_ref, b_ref, w_ref, o_ref, l_ref, t_ref, sem):
    flat = in_ref.reshape(in_ref.shape[0] * 16, 128)
    lane = lax.broadcasted_iota(jnp.int32, (128, 128), 1)

    def taken(c):
        return flat[pl.ds(c, 128, stride=16), :]

    def loaded(c):
        return jnp.concatenate([taken(c), taken(8 + c)], axis=1)

    samples = o_ref.shape[0] // spans
    copies = []
    for i in range(3):
        solved = full_dot(f_ref[...], loaded(i)) + full_dot(g_ref[...], loaded(3 + i))
        both = full_dot(b_ref[...], solved / d_ref[...])
        value, slope = both[:128], both[128:]
        t_ref[i, :, 0] = value[:, :128].reshape(spans, 8, 128)
        t_ref[i, :, 1] = slope[:, :128].reshape(spans, 8, 128)
        mixed = jnp.where(lane < 64, value[:, 128:], pltpu.roll(slope[:, 128:], 64, 1))
        t_ref[i, :, 2] = mixed.reshape(spans, 8, 128)
        for k in range(samples):
            copy = pltpu.make_async_copy(
                t_ref.at[i], o_ref.at[pl.ds(k * spans, spans), i], sem.at[i, k]
            )
            copy.start()
            copies.append(copy)

    def last(c):
        if c < 2:
            return taken(6 + c)
        first, second = taken(8 + 2 * (c - 2)), taken(9 + 2 * (c - 2))
        return jnp.where(lane < 64, pltpu.roll(first, 64, 1), second)

    for i in range(3):
        solved = full_dot(f_ref[...], last(i)) + full_dot(g_ref[...], last(3 + i))
        both = full_dot(w_ref[...], solved / e_ref[...])
        l_ref[i] = both[:8]
        l_ref[3 + i] = both[8:]
    for copy in copies:
        copy.wait()


def own_row(spectra, damping, last_damping, forward, forward_slope, inverse, slab_inverse, samples, spans):
    whole = pl.BlockSpec(memory_space=pltpu.VMEM)
    return pl.pallas_call(
        functools.partial(row_kernel, spans),
        in_specs=[whole] * 7,
        out_specs=(pl.BlockSpec(memory_space=pltpu.HBM), whole),
        out_shape=(
            pltpu.HBM((samples * spans, 3, 3, 8, 128), jnp.float32),
            jax.ShapeDtypeStruct((6, 8, 128), jnp.float32),
        ),
        scratch_shapes=[
            pltpu.VMEM((3, spans, 3, 8, 128), jnp.float32),
            pltpu.SemaphoreType.DMA((3, samples)),
        ],
        compiler_params=pltpu.CompilerParams(vmem_limit_bytes=32 * 1024 * 1024),
    )(spectra, damping, last_damping, forward, forward_slope, inverse, slab_inverse)


def slab_kernel(r_ref, l_ref, t_ref, c_ref, x_ref, b_ref, v_ref, g_ref):
    i = pl.program_id(0)
    rows = r_ref.shape[0]
    _, size_y, slab, size_x = v_ref.shape
    flat = r_ref.reshape(rows * 3 * slab, 128)
    column = jnp.broadcast_to(c_ref[...], (c_ref.shape[0], 128))
    out_v = v_ref.reshape(size_y * slab, size_x)
    out_g = g_ref.reshape(3, size_y * slab, size_x)
    lane = lax.broadcasted_iota(jnp.int32, (rows, 128), 1)
    half = t_ref.shape[0] // 2
    for first in range(0, slab, 2):
        values, slopes = [], []
        for z in (first, first + 1):
            value, slope, high = [
                flat[pl.ds(slab * part + z, rows, stride=3 * slab), :] for part in range(3)
            ]
            value_high = jnp.where(lane < 64, high, 0.0)
            slope_high = jnp.where(lane < 64, pltpu.roll(high, 64, 1), 0.0)
            values.append(jnp.concatenate([value, value_high], axis=1))
            slopes.append(jnp.concatenate([slope, slope_high], axis=1))
        across = (((1,), (1,)), ((), ()))
        value = lax.dot_general(
            t_ref[...],
            three_of(jnp.concatenate(values, axis=0), 1),
            across,
            preferred_element_type=jnp.float32,
        )
        slope = lax.dot_general(
            t_ref[:half],
            three_of(jnp.concatenate(slopes, axis=0), 1),
            across,
            preferred_element_type=jnp.float32,
        )
        for k, z in enumerate((first, first + 1)):
            place = pl.ds(z, size_y, stride=slab)
            lanes = slice(k * rows, k * rows + rows)
            value_z = value[:, lanes] + column * l_ref[i, pl.ds(z, 1), :]
            slope_z = slope[:, lanes] + column[:half] * l_ref[3 + i, pl.ds(z, 1), :]
            both = jnp.dot(
                three_of(value_z[:half], 1), x_ref[...], preferred_element_type=jnp.float32
            )
            out_v[place, :] = both[:size_y, :size_x]
            out_g[0, place, :] = both[:size_y, size_x:]
            both = jnp.dot(
                jnp.concatenate([three_of(value_z[half:], 1), three_of(slope_z, 1)], axis=1),
                b_ref[...],
                preferred_element_type=jnp.float32,
            )
            out_g[1, place, :] = both[:size_y, :size_x]
            out_g[2, place, :] = both[:size_y, size_x:]


def slab_values(rows, last, wall_table, last_column, table_x, table_pair, size_y):
    count = rows.shape[0]
    slab, size_x = rows.shape[3], table_x.shape[1] // 2
    whole = pl.BlockSpec(memory_space=pltpu.VMEM)

    return pl.pallas_call(
        slab_kernel,
        grid=(3,),
        in_specs=[
            pl.BlockSpec((count, 1, 3, slab, 128), lambda i: (0, i, 0, 0, 0)),
            whole,
            whole,
            whole,
            whole,
            whole,
        ],
        out_specs=(
            pl.BlockSpec((1, size_y, slab, size_x), lambda i: (i, 0, 0, 0)),
            pl.BlockSpec((3, size_y, slab, size_x), lambda i: (i, 0, 0, 0)),
        ),
        out_shape=(
            jax.ShapeDtypeStruct((3, size_y, slab, size_x), jnp.float32),
            jax.ShapeDtypeStruct((9, size_y, slab, size_x), jnp.float32),
        ),
        compiler_params=pltpu.CompilerParams(vmem_limit_bytes=60 * 1024 * 1024),
    )(rows, last, wall_table, last_column, table_x, table_pair)


def summed(planes, beside):
    count = lax.axis_size("sample")
    ring = count // 2
    index = lax.axis_index("sample")
    place = index % ring
    quarters = planes.reshape((ring, planes.shape[0] // ring) + planes.shape[1:])

    def shifted(values, k):
        pairs = [(i, i - i % ring + (i + k) % ring) for i in range(count)]
        return lax.ppermute(values, "sample", pairs)

    ahead = lax.dynamic_slice_in_dim(
        jnp.concatenate([quarters, quarters]), place, ring, axis=0
    )
    total = ahead[0]
    for part in [shifted(ahead[k], k) for k in range(1, ring)]:
        total = total + part
    pairs = [(i, (i + ring) % count) for i in range(count)]
    total = total + lax.ppermute(total, "sample", pairs)
    total, beside = lax.optimization_barrier((total, beside))
    parts = [shifted(total, k) for k in range(ring - 1, 0, -1)] + [total]
    start = (ring - 1 - place) % ring
    gathered = lax.dynamic_slice_in_dim(jnp.stack(parts + parts), start, ring, axis=0)
    return gathered.reshape(planes.shape), beside


def on_device(
    fields, wiener, velocity, gradient, wall_derivative, to_modes, from_modes, mode_rates
):
    size_x, slab, size_y = fields.shape[2:]
    samples = lax.axis_size("sample")
    spans = lax.axis_size("span")
    size_z = slab * spans
    step_x = LENGTH_X / size_x
    step_z = LENGTH_Z / size_z
    coupling = TIME_STEP * POLYMER_WEIGHT
    relax = TIME_STEP / (2.0 * WEISSENBERG)

    rows_x, slope_rows_x, square_x = real_basis(size_x, LENGTH_X)
    rows_z, slope_rows_z, square_z = real_basis(size_z, LENGTH_Z)
    order = np.array([slab * (d % spans) + d // spans for d in range(samples * spans)])

    field = jnp.transpose(fields[:, 0], (2, 0, 3, 1))
    ahead = [(i, (i + 1) % spans) for i in range(spans)]
    back = [((i + 1) % spans, i) for i in range(spans)]
    below = lax.ppermute(field[-1], "span", ahead)
    above = lax.ppermute(field[0], "span", back)
    speed = jnp.transpose(velocity, (0, 3, 2, 1))
    free = spring_free(
        field,
        jnp.transpose(wiener[:, 0], (0, 3, 2, 1)),
        speed,
        jnp.transpose(gradient, (0, 3, 2, 1)),
        below,
        above,
        wall_derivative,
        step_x,
        step_z,
    )
    total_square, free = summed(jnp.sum(field * field, axis=1), free)
    slab_spring = 1.0 / (1.0 - total_square / samples / EXTENSIBILITY)
    new_fields = free - relax * slab_spring[:, None] * field
    moved = lax.all_to_all(new_fields, "sample", 0, 0, tiled=True)

    own_velocity = lax.dynamic_index_in_dim(
        speed, lax.axis_index("sample"), 2, keepdims=False
    )
    modes = padded(to_modes, LANES, size_y)
    modes_slope = coupling * jnp.dot(modes, wall_derivative, precision=FULL)
    modes_velocity = jnp.einsum("my,cyx->cmx", modes, own_velocity, precision=FULL)
    modes_table = jnp.concatenate([coupling * modes, modes_slope])
    spring = lax.dynamic_index_in_dim(
        slab_spring, lax.axis_index("sample"), 0, keepdims=False
    )
    message = own_plane(
        moved,
        spring,
        modes_velocity,
        split_three(padded(modes_table, 2 * LANES, LANES), 1),
        f32(np.concatenate([rows_x, slope_rows_x @ rows_x], axis=1)),
    )
    spectra = lax.all_to_all(message, BOTH, 0, 0, tiled=True)

    row = lax.axis_index("sample") * spans + lax.axis_index("span")
    square_row = lax.dynamic_index_in_dim(f32(square_x), row, 0, keepdims=False)
    rates = padded(mode_rates[None, :], 1, LANES)
    damping = 1.0 + TIME_STEP * VISCOSITY * (
        square_row + f32(square_z)[:, None] + rates
    )
    last_damping = 1.0 + TIME_STEP * VISCOSITY * (
        f32(square_x)[None, :] + f32(square_z)[:, None] + mode_rates[size_y - 1]
    )
    inverse = np.stack([rows_z.T, rows_z.T @ slope_rows_z])
    slab_inverse = lax.dynamic_index_in_dim(
        f32(inverse.reshape(2, spans, slab, size_z)), lax.axis_index("span"), 1, keepdims=False
    ).reshape(2 * slab, size_z)
    back, last = own_row(
        spectra,
        damping,
        last_damping,
        f32(rows_z[:, order]),
        f32((slope_rows_z @ rows_z)[:, order]),
        f32(inverse.reshape(2 * size_z, size_z)),
        slab_inverse,
        samples,
        spans,
    )
    rows = lax.all_to_all(back, BOTH, 0, 0, tiled=True)

    modes_wall = jnp.dot(wall_derivative, from_modes, precision=FULL)
    wall_table = jnp.concatenate(
        [padded(from_modes, 208, LANES), padded(modes_wall, 208, LANES)]
    )
    new_velocity, new_gradient = slab_values(
        rows,
        last,
        split_three(wall_table.at[:, size_y - 1].set(0.0), 1),
        wall_table[:, size_y - 1 : size_y],
        stacked_three(np.concatenate([rows_x, (rows_x.T @ slope_rows_x).T], axis=1)),
        paired_three(rows_x),
        size_y,
    )
    return (
        jnp.transpose(new_fields, (1, 3, 0, 2))[:, None],
        jnp.transpose(new_velocity, (0, 3, 2, 1)),
        jnp.transpose(new_gradient, (0, 3, 2, 1)),
    )


def solution(mesh):
    in_specs = (
        P(None, "sample", None, "span", None),
        P(None, "sample", None, "span", None),
        P(None, None, "span", None),
        P(None, None, "span", None),
        P(),
        P(),
        P(),
        P(),
    )
    out_specs = (
        P(None, "sample", None, "span", None),
        P(None, None, "span", None),
        P(None, None, "span", None),
    )
    return jax.shard_map(
        on_device, mesh=mesh, in_specs=in_specs, out_specs=out_specs, check_vma=False
    )
```

```python
import functools
import math

import jax
import jax.numpy as jnp
import numpy as np
from jax import lax
from jax.experimental import pallas as pl
from jax.experimental.pallas import tpu as pltpu
from jax.sharding import PartitionSpec as P

TIME_STEP = 0.01
WEISSENBERG = 0.05
EXTENSIBILITY = 10.0
POLYMER_WEIGHT = 5.0
VISCOSITY = 0.5
DIFFUSIVITY = 0.003
LENGTH_X = math.pi
LENGTH_Z = 2.0 * math.pi / 3.0
FULL = lax.Precision.HIGHEST
HIGH = lax.Precision.HIGH
BOTH = ("sample", "span")
LANES = 256
PAIRS = ((0, 0), (0, 1), (0, 2), (1, 1), (1, 2), (2, 2))
COLUMN = ((0, 1, 2), (1, 3, 4), (2, 4, 5))


def real_basis(count, extent):
    half = count // 2
    place = np.arange(count)
    rows = np.zeros((count, count))
    kappa = np.zeros(count)
    slope = np.zeros((count, count))
    unit = 2.0 * math.pi / extent
    rows[0] = math.sqrt(1.0 / count)
    for k in range(1, half):
        angle = 2.0 * math.pi * ((k * place) % count) / count
        rows[k] = math.sqrt(2.0 / count) * np.cos(angle)
        rows[half + k] = math.sqrt(2.0 / count) * np.sin(angle)
        kappa[k] = kappa[half + k] = unit * k
        slope[k, half + k] = unit * k
        slope[half + k, k] = -unit * k
    rows[half] = math.sqrt(1.0 / count) * (1.0 - 2.0 * (place % 2))
    kappa[half] = unit * half
    return rows, slope, kappa * kappa


def f32(values):
    return jnp.asarray(np.asarray(values, np.float32))


def slope_kernel(f_ref, d_ref, e_ref, o_ref):
    size_x = f_ref.shape[3]
    for i in range(3):
        pair = jnp.concatenate([f_ref[0, i], f_ref[1, i]], axis=1)
        high = pair.astype(jnp.bfloat16)
        low = (pair - high.astype(jnp.float32)).astype(jnp.bfloat16)
        slope = jnp.dot(d_ref[...], high, preferred_element_type=jnp.float32)
        slope += jnp.dot(d_ref[...], low, preferred_element_type=jnp.float32)
        slope += jnp.dot(e_ref[...], high, preferred_element_type=jnp.float32)
        o_ref[0, i] = slope[:, :size_x]
        o_ref[1, i] = slope[:, size_x:]


def wall_slope(planes, wall_derivative):
    slab, _, size_y, size_x = planes.shape
    high = lax.reduce_precision(wall_derivative, 8, 7)
    low = (wall_derivative - high).astype(jnp.bfloat16)
    whole = pl.BlockSpec(memory_space=pltpu.VMEM)
    pair = pl.BlockSpec((2, 3, size_y, size_x), lambda j: (j, 0, 0, 0))
    return pl.pallas_call(
        slope_kernel,
        grid=(slab // 2,),
        in_specs=[pair, whole, whole],
        out_specs=pair,
        out_shape=pltpu.HBM(planes.shape, jnp.float32),
        compiler_params=pltpu.CompilerParams(vmem_limit_bytes=24 * 1024 * 1024),
        cost_estimate=pl.CostEstimate(flops=10**9, bytes_accessed=6 * 10**6, transcendentals=0),
    )(planes, high.astype(jnp.bfloat16), low)


def free_kernel(scales, p_ref, s_ref, w_ref, v_ref, g_ref, lo_ref, hi_ref, o_ref):
    scale_x, scale_z, scale_c, scale_w = scales
    slab, _, block, size_x = p_ref.shape
    noise, speed, tensor = [
        r.reshape(r.shape[0], block * slab, size_x) for r in (w_ref, v_ref, g_ref)
    ]
    for z in range(slab):
        plane = pl.ds(z, block, stride=slab)
        speed_x, speed_y, speed_z = [speed[c, plane, :] for c in range(3)]
        parts = [p_ref[z, c] for c in range(3)]
        for i in range(3):
            own = parts[i]
            upper = hi_ref[i] if z == slab - 1 else p_ref[z + 1, i]
            lower = lo_ref[i] if z == 0 else p_ref[z - 1, i]
            slope_x = pltpu.roll(own, size_x - 1, 1) - pltpu.roll(own, 1, 1)
            advect = (
                speed_x * (scale_x * slope_x)
                + speed_y * s_ref[z, i]
                + speed_z * (scale_z * (upper - lower))
            )
            stretch = (
                tensor[3 * i, plane, :] * parts[0]
                + tensor[3 * i + 1, plane, :] * parts[1]
                + tensor[3 * i + 2, plane, :] * parts[2]
            )
            result = own + TIME_STEP * (stretch - advect)
            result = result + scale_c * (upper - 2.0 * own + lower)
            o_ref[z, i] = result + scale_w * noise[i, plane, :]


def spring_free(planes, slope, wiener, velocity, gradient, below, above, step_x, step_z):
    slab, _, size_y, size_x = planes.shape
    block = 40
    scales = (
        1.0 / (2.0 * step_x),
        1.0 / (2.0 * step_z),
        DIFFUSIVITY * TIME_STEP / (step_z * step_z),
        math.sqrt(TIME_STEP / WEISSENBERG),
    )

    def rows(count):
        return pl.BlockSpec((count, block, slab, size_x), lambda j: (0, j, 0, 0))

    across = pl.BlockSpec((slab, 3, block, size_x), lambda j: (0, 0, j, 0))
    edge = pl.BlockSpec((3, block, size_x), lambda j: (0, j, 0))
    return pl.pallas_call(
        functools.partial(free_kernel, scales),
        grid=(-(-size_y // block),),
        in_specs=[across, across, rows(3), rows(3), rows(9), edge, edge],
        out_specs=across,
        out_shape=pltpu.HBM(planes.shape, jnp.float32),
        compiler_params=pltpu.CompilerParams(vmem_limit_bytes=60 * 1024 * 1024),
        cost_estimate=pl.CostEstimate(flops=10**8, bytes_accessed=19 * 10**6, transcendentals=0),
    )(planes, slope, wiener, velocity, gradient, below, above)


def padded(values, rows, columns):
    return jnp.pad(
        values, ((0, rows - values.shape[0]), (0, columns - values.shape[1]))
    )


def stacked_three(table):
    table = np.asarray(table, np.float32)
    high = table.astype(jnp.bfloat16)
    low = (table - high.astype(np.float32)).astype(jnp.bfloat16)
    return jnp.asarray(np.concatenate([high, high, low], axis=0))


def paired_three(table):
    table = np.asarray(table, np.float32)
    high = table.astype(jnp.bfloat16)
    low = (table - high.astype(np.float32)).astype(jnp.bfloat16)
    column = np.concatenate([high, high, low], axis=0)
    empty = np.zeros_like(column)
    return jnp.asarray(
        np.concatenate(
            [np.concatenate([column, empty], axis=1), np.concatenate([empty, column], axis=1)]
        )
    )


def split_three(table, axis):
    high = lax.reduce_precision(table, 8, 7)
    low = (table - high).astype(jnp.bfloat16)
    high = high.astype(jnp.bfloat16)
    return jnp.concatenate([high, high, low], axis=axis)


def three_of(values, axis):
    high = values.astype(jnp.bfloat16)
    low = (values - high.astype(jnp.float32)).astype(jnp.bfloat16)
    return jnp.concatenate([high, low, high], axis=axis)


def full_dot(a, b, side=0):
    return lax.dot_general(
        a,
        b,
        (((1,), (side,)), ((), ())),
        precision=FULL,
        preferred_element_type=jnp.float32,
    )


def plane_kernel(n_ref, s_ref, v_ref, m_ref, x_ref, o_ref, t_ref):
    k = pl.program_id(0)
    steps = pl.num_programs(0)
    count = steps * n_ref.shape[0]
    size_y, size_x = s_ref.shape

    @pl.when(k == 0)
    def _():
        t_ref[...] = jnp.zeros_like(t_ref)

    for start in range(0, size_y, 32):
        part = pl.ds(start, min(32, size_y - start))
        moved = [[n_ref[f, c, part, :] for c in range(3)] for f in range(n_ref.shape[0])]
        for p, (i, j) in enumerate(PAIRS):
            value = moved[0][i] * moved[0][j]
            for own in moved[1:]:
                value += own[i] * own[j]
            t_ref[p, part, :] += value

    @pl.when(k == steps - 1)
    def _():
        for start in range(0, size_y, 64):
            part = pl.ds(start, min(64, size_y - start))
            spring = s_ref[part, :]
            for p, (i, j) in enumerate(PAIRS):
                value = spring * (t_ref[p, part, :] / count)
                t_ref[p, part, :] = value - 1.0 if i == j else value
        scaled, slope = m_ref[:LANES, :], m_ref[LANES:, :]
        last_mode = size_y - 1
        rest = [None] * 6
        for i in range(3):
            column = [t_ref[p] for p in COLUMN[i]]
            direct = v_ref[i] + jnp.dot(
                slope, three_of(column[1], 0), preferred_element_type=jnp.float32
            )
            along = jnp.dot(
                scaled,
                three_of(jnp.concatenate([column[0], column[2]], axis=1), 0),
                preferred_element_type=jnp.float32,
            )
            force = full_dot(
                x_ref[...], jnp.concatenate([direct, along[:, :size_x]], axis=1), 1
            )
            force_z = full_dot(x_ref[:, :size_x], along[:, size_x:], 1)
            top = slice(last_mode, last_mode + 8)
            own = jnp.concatenate([direct[top], along[top, :size_x]], axis=1)
            rest[i] = full_dot(own, x_ref[...], 1)[:1]
            rest[3 + i] = full_dot(along[top, size_x:], x_ref[:, :size_x], 1)[:1]
            for half in range(2):
                lanes = slice(half * 128, half * 128 + 128)
                o_ref[pl.ds(8 * half + i, 128, stride=16), :] = force[:, lanes]
                o_ref[pl.ds(8 * half + 3 + i, 128, stride=16), :] = force_z[:, lanes]
        lane = lax.broadcasted_iota(jnp.int32, (128, 128), 1)
        for c in range(2):
            o_ref[pl.ds(6 + c, 128, stride=16), :] = jnp.broadcast_to(rest[c], (128, 128))
        for c in range(4):
            for part in range(2):
                row = jnp.broadcast_to(rest[2 + c], (128, 128))
                row = row if part else pltpu.roll(row, 64, 1)
                place = pl.ds(8 + 2 * c + part, 128, stride=16)
                kept = o_ref[place, :] if 2 * c + part < 6 else jnp.zeros_like(row)
                o_ref[place, :] = jnp.where(lane < 64, kept, row)


def own_plane(moved, spring, modes_velocity, modes, rows):
    count, _, size_y, size_x = moved.shape
    whole = pl.BlockSpec(memory_space=pltpu.VMEM)
    message = pl.pallas_call(
        plane_kernel,
        grid=(2,),
        in_specs=[
            pl.BlockSpec((count // 2, 3, size_y, size_x), lambda k: (k, 0, 0, 0)),
            whole,
            whole,
            whole,
            whole,
        ],
        out_specs=pl.BlockSpec((size_x * 16, 128), lambda k: (0, 0)),
        out_shape=jax.ShapeDtypeStruct((size_x * 16, 128), jnp.float32),
        scratch_shapes=[pltpu.VMEM((6, LANES, size_x), jnp.float32)],
        compiler_params=pltpu.CompilerParams(vmem_limit_bytes=24 * 1024 * 1024),
    )(moved, spring, modes_velocity, modes, rows)
    return message.reshape(size_x, 2, 8, 128)


def row_kernel(spans, in_ref, d_ref, e_ref, f_ref, g_ref, b_ref, w_ref, o_ref, l_ref, t_ref, sem):
    flat = in_ref.reshape(in_ref.shape[0] * 16, 128)
    lane = lax.broadcasted_iota(jnp.int32, (128, 128), 1)

    def taken(c):
        return flat[pl.ds(c, 128, stride=16), :]

    def loaded(c):
        return jnp.concatenate([taken(c), taken(8 + c)], axis=1)

    samples = o_ref.shape[0] // spans
    copies = []
    for i in range(3):
        solved = full_dot(f_ref[...], loaded(i)) + full_dot(g_ref[...], loaded(3 + i))
        both = full_dot(b_ref[...], solved / d_ref[...])
        value, slope = both[:128], both[128:]
        t_ref[i, :, 0] = value[:, :128].reshape(spans, 8, 128)
        t_ref[i, :, 1] = slope[:, :128].reshape(spans, 8, 128)
        mixed = jnp.where(lane < 64, value[:, 128:], pltpu.roll(slope[:, 128:], 64, 1))
        t_ref[i, :, 2] = mixed.reshape(spans, 8, 128)
        for k in range(samples):
            copy = pltpu.make_async_copy(
                t_ref.at[i], o_ref.at[pl.ds(k * spans, spans), i], sem.at[i, k]
            )
            copy.start()
            copies.append(copy)

    def last(c):
        if c < 2:
            return taken(6 + c)
        first, second = taken(8 + 2 * (c - 2)), taken(9 + 2 * (c - 2))
        return jnp.where(lane < 64, pltpu.roll(first, 64, 1), second)

    for i in range(3):
        solved = full_dot(f_ref[...], last(i)) + full_dot(g_ref[...], last(3 + i))
        both = full_dot(w_ref[...], solved / e_ref[...])
        l_ref[i] = both[:8]
        l_ref[3 + i] = both[8:]
    for copy in copies:
        copy.wait()


def own_row(spectra, damping, last_damping, forward, forward_slope, inverse, slab_inverse, samples, spans):
    whole = pl.BlockSpec(memory_space=pltpu.VMEM)
    return pl.pallas_call(
        functools.partial(row_kernel, spans),
        in_specs=[whole] * 7,
        out_specs=(pl.BlockSpec(memory_space=pltpu.HBM), whole),
        out_shape=(
            pltpu.HBM((samples * spans, 3, 3, 8, 128), jnp.float32),
            jax.ShapeDtypeStruct((6, 8, 128), jnp.float32),
        ),
        scratch_shapes=[
            pltpu.VMEM((3, spans, 3, 8, 128), jnp.float32),
            pltpu.SemaphoreType.DMA((3, samples)),
        ],
        compiler_params=pltpu.CompilerParams(vmem_limit_bytes=32 * 1024 * 1024),
    )(spectra, damping, last_damping, forward, forward_slope, inverse, slab_inverse)


def slab_kernel(r_ref, l_ref, t_ref, c_ref, x_ref, b_ref, v_ref, g_ref):
    i = pl.program_id(0)
    rows = r_ref.shape[0]
    _, size_y, slab, size_x = v_ref.shape
    flat = r_ref.reshape(rows * 3 * slab, 128)
    column = jnp.broadcast_to(c_ref[...], (c_ref.shape[0], 128))
    out_v = v_ref.reshape(size_y * slab, size_x)
    out_g = g_ref.reshape(3, size_y * slab, size_x)
    lane = lax.broadcasted_iota(jnp.int32, (rows, 128), 1)
    half = t_ref.shape[0] // 2
    for first in range(0, slab, 2):
        values, slopes = [], []
        for z in (first, first + 1):
            value, slope, high = [
                flat[pl.ds(slab * part + z, rows, stride=3 * slab), :] for part in range(3)
            ]
            value_high = jnp.where(lane < 64, high, 0.0)
            slope_high = jnp.where(lane < 64, pltpu.roll(high, 64, 1), 0.0)
            values.append(jnp.concatenate([value, value_high], axis=1))
            slopes.append(jnp.concatenate([slope, slope_high], axis=1))
        across = (((1,), (1,)), ((), ()))
        value = lax.dot_general(
            t_ref[...],
            three_of(jnp.concatenate(values, axis=0), 1),
            across,
            preferred_element_type=jnp.float32,
        )
        slope = lax.dot_general(
            t_ref[:half],
            three_of(jnp.concatenate(slopes, axis=0), 1),
            across,
            preferred_element_type=jnp.float32,
        )
        for k, z in enumerate((first, first + 1)):
            place = pl.ds(z, size_y, stride=slab)
            lanes = slice(k * rows, k * rows + rows)
            value_z = value[:, lanes] + column * l_ref[i, pl.ds(z, 1), :]
            slope_z = slope[:, lanes] + column[:half] * l_ref[3 + i, pl.ds(z, 1), :]
            both = jnp.dot(
                three_of(value_z[:half], 1), x_ref[...], preferred_element_type=jnp.float32
            )
            out_v[place, :] = both[:size_y, :size_x]
            out_g[0, place, :] = both[:size_y, size_x:]
            both = jnp.dot(
                jnp.concatenate([three_of(value_z[half:], 1), three_of(slope_z, 1)], axis=1),
                b_ref[...],
                preferred_element_type=jnp.float32,
            )
            out_g[1, place, :] = both[:size_y, :size_x]
            out_g[2, place, :] = both[:size_y, size_x:]


def slab_values(rows, last, wall_table, last_column, table_x, table_pair, size_y):
    count = rows.shape[0]
    slab, size_x = rows.shape[3], table_x.shape[1] // 2
    whole = pl.BlockSpec(memory_space=pltpu.VMEM)

    return pl.pallas_call(
        slab_kernel,
        grid=(3,),
        in_specs=[
            pl.BlockSpec((count, 1, 3, slab, 128), lambda i: (0, i, 0, 0, 0)),
            whole,
            whole,
            whole,
            whole,
            whole,
        ],
        out_specs=(
            pl.BlockSpec((1, size_y, slab, size_x), lambda i: (i, 0, 0, 0)),
            pl.BlockSpec((3, size_y, slab, size_x), lambda i: (i, 0, 0, 0)),
        ),
        out_shape=(
            jax.ShapeDtypeStruct((3, size_y, slab, size_x), jnp.float32),
            jax.ShapeDtypeStruct((9, size_y, slab, size_x), jnp.float32),
        ),
        compiler_params=pltpu.CompilerParams(vmem_limit_bytes=60 * 1024 * 1024),
    )(rows, last, wall_table, last_column, table_x, table_pair)


def summed(planes, early, rest):
    count = lax.axis_size("sample")
    ring = count // 2
    index = lax.axis_index("sample")
    place = index % ring
    quarters = planes.reshape((ring, planes.shape[0] // ring) + planes.shape[1:])

    def shifted(values, k):
        pairs = [(i, i - i % ring + (i + k) % ring) for i in range(count)]
        return lax.ppermute(values, "sample", pairs)

    ahead = lax.dynamic_slice_in_dim(
        jnp.concatenate([quarters, quarters]), place, ring, axis=0
    )
    total = ahead[0]
    for part in [shifted(ahead[k], k) for k in range(1, ring)]:
        total = total + part
    total, early = lax.optimization_barrier((total, early))
    pairs = [(i, (i + ring) % count) for i in range(count)]
    total = total + lax.ppermute(total, "sample", pairs)
    total, beside = lax.optimization_barrier((total, rest(early)))
    parts = [shifted(total, k) for k in range(ring - 1, 0, -1)] + [total]
    start = (ring - 1 - place) % ring
    gathered = lax.dynamic_slice_in_dim(jnp.stack(parts + parts), start, ring, axis=0)
    return gathered.reshape(planes.shape), beside


def on_device(
    fields, wiener, velocity, gradient, wall_derivative, to_modes, from_modes, mode_rates
):
    size_x, slab, size_y = fields.shape[2:]
    samples = lax.axis_size("sample")
    spans = lax.axis_size("span")
    size_z = slab * spans
    step_x = LENGTH_X / size_x
    step_z = LENGTH_Z / size_z
    coupling = TIME_STEP * POLYMER_WEIGHT
    relax = TIME_STEP / (2.0 * WEISSENBERG)

    rows_x, slope_rows_x, square_x = real_basis(size_x, LENGTH_X)
    rows_z, slope_rows_z, square_z = real_basis(size_z, LENGTH_Z)
    order = np.array([slab * (d % spans) + d // spans for d in range(samples * spans)])

    field = jnp.transpose(fields[:, 0], (2, 0, 3, 1))
    ahead = [(i, (i + 1) % spans) for i in range(spans)]
    back = [((i + 1) % spans, i) for i in range(spans)]
    below = lax.ppermute(field[-1], "span", ahead)
    above = lax.ppermute(field[0], "span", back)
    speed = jnp.transpose(velocity, (0, 3, 2, 1))
    def rest(slope):
        return spring_free(
            field,
            slope,
            jnp.transpose(wiener[:, 0], (0, 3, 2, 1)),
            speed,
            jnp.transpose(gradient, (0, 3, 2, 1)),
            below,
            above,
            step_x,
            step_z,
        )

    slope = wall_slope(field, wall_derivative)
    total_square, free = summed(jnp.sum(field * field, axis=1), slope, rest)
    slab_spring = 1.0 / (1.0 - total_square / samples / EXTENSIBILITY)
    new_fields = free - relax * slab_spring[:, None] * field
    moved = lax.all_to_all(new_fields, "sample", 0, 0, tiled=True)

    own_velocity = lax.dynamic_index_in_dim(
        speed, lax.axis_index("sample"), 2, keepdims=False
    )
    modes = padded(to_modes, LANES, size_y)
    modes_slope = coupling * jnp.dot(modes, wall_derivative, precision=FULL)
    modes_velocity = jnp.einsum("my,cyx->cmx", modes, own_velocity, precision=FULL)
    modes_table = jnp.concatenate([coupling * modes, modes_slope])
    spring = lax.dynamic_index_in_dim(
        slab_spring, lax.axis_index("sample"), 0, keepdims=False
    )
    message = own_plane(
        moved,
        spring,
        modes_velocity,
        split_three(padded(modes_table, 2 * LANES, LANES), 1),
        f32(np.concatenate([rows_x, slope_rows_x @ rows_x], axis=1)),
    )
    spectra = lax.all_to_all(message, BOTH, 0, 0, tiled=True)

    row = lax.axis_index("sample") * spans + lax.axis_index("span")
    square_row = lax.dynamic_index_in_dim(f32(square_x), row, 0, keepdims=False)
    rates = padded(mode_rates[None, :], 1, LANES)
    damping = 1.0 + TIME_STEP * VISCOSITY * (
        square_row + f32(square_z)[:, None] + rates
    )
    last_damping = 1.0 + TIME_STEP * VISCOSITY * (
        f32(square_x)[None, :] + f32(square_z)[:, None] + mode_rates[size_y - 1]
    )
    inverse = np.stack([rows_z.T, rows_z.T @ slope_rows_z])
    slab_inverse = lax.dynamic_index_in_dim(
        f32(inverse.reshape(2, spans, slab, size_z)), lax.axis_index("span"), 1, keepdims=False
    ).reshape(2 * slab, size_z)
    back, last = own_row(
        spectra,
        damping,
        last_damping,
        f32(rows_z[:, order]),
        f32((slope_rows_z @ rows_z)[:, order]),
        f32(inverse.reshape(2 * size_z, size_z)),
        slab_inverse,
        samples,
        spans,
    )
    rows = lax.all_to_all(back, BOTH, 0, 0, tiled=True)

    modes_wall = jnp.dot(wall_derivative, from_modes, precision=FULL)
    wall_table = jnp.concatenate(
        [padded(from_modes, 208, LANES), padded(modes_wall, 208, LANES)]
    )
    new_velocity, new_gradient = slab_values(
        rows,
        last,
        split_three(wall_table.at[:, size_y - 1].set(0.0), 1),
        wall_table[:, size_y - 1 : size_y],
        stacked_three(np.concatenate([rows_x, (rows_x.T @ slope_rows_x).T], axis=1)),
        paired_three(rows_x),
        size_y,
    )
    return (
        jnp.transpose(new_fields, (1, 3, 0, 2))[:, None],
        jnp.transpose(new_velocity, (0, 3, 2, 1)),
        jnp.transpose(new_gradient, (0, 3, 2, 1)),
    )


def solution(mesh):
    in_specs = (
        P(None, "sample", None, "span", None),
        P(None, "sample", None, "span", None),
        P(None, None, "span", None),
        P(None, None, "span", None),
        P(),
        P(),
        P(),
        P(),
    )
    out_specs = (
        P(None, "sample", None, "span", None),
        P(None, None, "span", None),
        P(None, None, "span", None),
    )
    return jax.shard_map(
        on_device, mesh=mesh, in_specs=in_specs, out_specs=out_specs, check_vma=False
    )
```
